256 devices in a mesh: tile: 64 (over z, y, core), frame: 4 (over x).
Axes of the slice: x: 4, y: 4, z: 8, core: 2. Of those that a mesh axis runs over, the one named last changes fastest.
Arguments:
- feats: bfloat16 [4, 16384, 256], P('frame', 'tile'), may hold values from -6 to 6
- routes: int32 [4, 64, 64], P('frame'), may hold values from 0 to 63, as said below
- interp: bfloat16 [4, 64, 16384, 128], P('frame', None, 'tile'), may hold values from -0.5 to 0.5
- w_value: bfloat16 [256, 256], replicated, may hold values from -0.375 to 0.375
- w_attn: bfloat16 [256, 64], replicated, may hold values from -48 to 48
- w_out: bfloat16 [256, 256], replicated, may hold values from -0.375 to 0.375
- grad_out: bfloat16 [4, 16384, 256], P('frame', 'tile'), may hold values from -6 to 6
Outputs:
- grad_feats: bfloat16 [4, 16384, 256], P('frame', 'tile')
- grad_w_value: float32 [256, 256], replicated
- grad_w_attn: float32 [256, 64], replicated
- grad_w_out: float32 [256, 256], replicated
The draws below stay inside these ranges and needn't reach their ends.
Inputs may be any that keep to these rules, and one draw needn't show every extreme that they name: `routes`: within one frame a reader tile names any one owner tile in at most 2 of its 64 columns; in every frame some owner tile is named in exactly 2 columns by every reader tile.
All inputs are finite; a program needn't handle non-finite values.
Results may differ from the reference program's by a relative error of at most 0.022.
Values may be sent and summed in bfloat16 or wider, within the bound.
A program may use at most 128 MiB of HBM per device.

```python
import math
import jax
import jax.numpy as jnp
from jax import lax

D = 256
H = 8
L = 2
P_SIZE = 4
CS = 128
HD = 32
HLP = 64
Q = 256
FRAMES = 4
CAP = 2
N_TILE = 64


def draw_routes(key, part):
    key_hot, key_rows = jax.random.split(key)
    hot_owner = jax.random.randint(key_hot, (FRAMES,), 0, N_TILE)
    pool_owners = jnp.repeat(jnp.arange(N_TILE - 1, dtype=jnp.int32), CAP)
    hot_rows = jnp.repeat(hot_owner, N_TILE)
    row_keys = jax.random.split(key_rows, FRAMES * N_TILE)

    def one_row(row_key, hot_value):
        key_pool, key_order = jax.random.split(row_key)
        others = jax.random.permutation(key_pool, pool_owners)[:HLP - CAP]
        others = others + (others >= hot_value).astype(jnp.int32)
        entries = jnp.concatenate([jnp.full((CAP,), hot_value, jnp.int32), others.astype(jnp.int32)])
        return jax.random.permutation(key_order, entries)
    rows_drawn = jax.vmap(one_row)(row_keys, hot_rows)
    return rows_drawn.reshape(FRAMES, N_TILE, HLP).astype(jnp.int32)


def draw_w_attn(key, part):
    key_base = jax.random.fold_in(key, 0)
    weights = jax.random.normal(key_base, (D, HLP), jnp.float32) / math.sqrt(D)
    return weights.astype(jnp.bfloat16)


def shard_levels(own_key, dims, pieces, low, high):
    level, own = 1.0, jax.random.fold_in(own_key, 6)
    for dim, parts in pieces:
        draws = jnp.exp(jax.random.uniform(jax.random.fold_in(own, dim), (parts,), jnp.float32, low / len(pieces), high / len(pieces)))
        level = level * jnp.repeat(draws, dims[dim] // parts).reshape([-1 if axis == dim else 1 for axis in range(len(dims))])
    return level


def centred(key, dims, spread, limit, pieces=(), kind=jnp.bfloat16):
    values = spread * jax.random.normal(key, dims, jnp.float32)
    if pieces:
        values = values * shard_levels(key, dims, pieces, -0.22, 0.18)
    return jnp.clip(values, -limit, limit).astype(kind)


def setup_inputs(seed: int = 0) -> dict:
    keys = jax.random.split(jax.random.key(seed), 8)
    feats = centred(keys[0], (FRAMES, N_TILE * Q, D), 1.0, 6.0, ((0, 4), (1, 64)))
    routes = draw_routes(jax.random.fold_in(keys[7], 71), 0)
    interp = centred(keys[2], (FRAMES, HLP, N_TILE * Q, CS), CS ** -0.5, 0.5, ((0, 4), (2, 64)))
    w_value = centred(keys[3], (D, D), D ** -0.5, 0.375)
    w_attn = draw_w_attn(jax.random.fold_in(keys[7], 71), 0)
    w_out = centred(keys[5], (D, D), D ** -0.5, 0.375)
    grad_out = centred(keys[6], (FRAMES, N_TILE * Q, D), 1.0, 6.0, ((0, 4), (1, 64)))
    return {"feats": feats, "routes": routes, "interp": interp, "w_value": w_value, "w_attn": w_attn, "w_out": w_out, "grad_out": grad_out}


def reference(feats, routes, interp, w_value, w_attn, w_out, grad_out):
    column = jnp.arange(HLP, dtype=jnp.int32)
    head_of = column // (L * P_SIZE)
    level_of = column // P_SIZE % L
    factor = 1.0 / math.sqrt(FRAMES * N_TILE * Q)
    grad_frames = []
    total_value = jnp.zeros((D, D), jnp.float32)
    total_attn = jnp.zeros((D, HLP), jnp.float32)
    total_out = jnp.zeros((D, D), jnp.float32)
    for frame_index in range(FRAMES):
        inputs_now = feats[frame_index]
        grads_now = grad_out[frame_index]
        weights_now = interp[frame_index]
        routes_now = routes[frame_index]
        values = jnp.dot(inputs_now, w_value, preferred_element_type=jnp.float32).astype(jnp.bfloat16)
        lookup = values.reshape(N_TILE, L, CS, H, HD).transpose(0, 1, 3, 4, 2)

        def reader(carried, reader_index):
            grad_lookup, part_attn, part_out = carried
            row_start = reader_index * Q
            rows_in = lax.dynamic_slice_in_dim(inputs_now, row_start, Q, 0)
            rows_grad = lax.dynamic_slice_in_dim(grads_now, row_start, Q, 0)
            tile_weights = lax.dynamic_slice_in_dim(weights_now, row_start, Q, 1)
            owners = routes_now[reader_index]
            fetched = lookup[owners, level_of, head_of]
            sampled = jnp.einsum('jdc,jqc->jdq', fetched.astype(jnp.float32), tile_weights.astype(jnp.float32))
            logits = jnp.dot(rows_in, w_attn, preferred_element_type=jnp.float32)
            attn = jax.nn.softmax(logits.reshape(Q, H, L * P_SIZE), axis=-1).reshape(Q, HLP)
            attn_heads = attn.T.reshape(H, L * P_SIZE, 1, Q)
            sampled_heads = sampled.reshape(H, L * P_SIZE, HD, Q)
            mixed = lax.optimization_barrier(jnp.sum(attn_heads * sampled_heads, axis=1)).reshape(D, Q).T.astype(jnp.bfloat16)
            grad_mixed = jnp.dot(rows_grad, w_out.T, preferred_element_type=jnp.float32)
            grad_mixed_heads = grad_mixed.T.reshape(H, 1, HD, Q)
            grad_attn = lax.optimization_barrier(jnp.sum(grad_mixed_heads * sampled_heads, axis=2)).reshape(HLP, Q).T.reshape(Q, H, L * P_SIZE)
            attn_query = attn.reshape(Q, H, L * P_SIZE)
            inner_term = lax.optimization_barrier(jnp.sum(attn_query * grad_attn, axis=-1, keepdims=True))
            grad_logits = (attn_query * (grad_attn - inner_term)).reshape(Q, HLP).astype(jnp.bfloat16)
            grad_sampled = (attn_heads * grad_mixed_heads).reshape(HLP, HD, Q).astype(jnp.bfloat16)
            contrib = jnp.einsum('jdq,jqc->jdc', grad_sampled.astype(jnp.float32), tile_weights.astype(jnp.float32))
            grad_lookup = grad_lookup.at[owners, level_of, head_of].add(contrib)
            grad_query = jnp.dot(grad_logits, w_attn.T, preferred_element_type=jnp.float32)
            part_attn = part_attn + jnp.dot(rows_in.T, grad_logits, preferred_element_type=jnp.float32)
            part_out = part_out + jnp.dot(mixed.T, rows_grad, preferred_element_type=jnp.float32)
            return ((grad_lookup, part_attn, part_out), grad_query)
        start_state = (jnp.zeros((N_TILE, L, H, HD, CS), jnp.float32), jnp.zeros((D, HLP), jnp.float32), jnp.zeros((D, D), jnp.float32))
        final_state, grad_query = lax.scan(reader, start_state, jnp.arange(N_TILE, dtype=jnp.int32))
        grad_lookup, part_attn, part_out = final_state
        grad_values = grad_lookup.transpose(0, 1, 4, 2, 3).reshape(N_TILE * Q, D).astype(jnp.bfloat16)
        grad_inputs = grad_query.reshape(N_TILE * Q, D) + jnp.dot(grad_values, w_value.T, preferred_element_type=jnp.float32)
        grad_frames.append(grad_inputs.astype(jnp.bfloat16))
        total_value = total_value + jnp.dot(inputs_now.T, grad_values, preferred_element_type=jnp.float32)
        total_attn = total_attn + part_attn
        total_out = total_out + part_out
    return (jnp.stack(grad_frames), total_value * factor, total_attn * factor, total_out * factor)
```

```python
import math

import jax
import jax.numpy as jnp
from jax import lax
from jax.experimental import pallas as pl
from jax.experimental.pallas import tpu as pltpu
from jax.sharding import PartitionSpec as P

MESH = pl.DeviceIdType.MESH
F32 = jnp.float32
BF16 = jnp.bfloat16
NZ = 8
NP = 8
NX = 4
H = 8
HALF = 2048
SHARE = 144
NN = (((1,), (0,)), ((), ()))
NT = (((1,), (1,)), ((), ()))


def dot(a, b, dims=NN):
    return lax.dot_general(a, b, dims, preferred_element_type=F32)


def block(index, size):
    return pl.ds(pl.multiple_of(index * size, size), size)


def kernel(
    feats, routes, interp, w_value, w_attn_t, w_out, grad_out,
    grad_feats, grad_w_value, grad_w_attn_t, grad_w_out,
    itp, v_rows, ag, send_f, recv_f, send_r, recv_r, acc,
    rs_send, rs_recv, con, con_rows, fet, attn_s, gm_s, ga_s, mixed_s, feats_t,
    pick_f, pick_r, mine_t, mine, route_s, gv_rows,
    rp_send, rp_recv, share_s, rz_send, rz_recv, rx_recv, gz, gp,
    itp_sem, bar_unused, ag_send_sem, ag_recv_sem, f_send_sem, f_recv_sem,
    r_send_sem, r_recv_sem, rs_send_sem, rs_recv_sem,
    p_send_sem, p_recv_sem, z_send_sem, z_recv_sem, x_send_sem, x_recv_sem,
    gz_send_sem, gz_recv_sem, gp_send_sem, gp_recv_sem,
):
    t = lax.axis_index("tile")
    f = lax.axis_index("frame")
    z = lax.div(t, NP)
    p = lax.rem(t, NP)

    def plane_tile(i):
        return z * NP + lax.rem(p + i, NP)

    def column_tile(i):
        return lax.rem(z + i, NZ) * NP + p

    right = column_tile(1)
    left = column_tile(NZ - 1)

    def remote(src, dst, send_sem, recv_sem, tile, frame):
        return pltpu.make_async_remote_copy(
            src_ref=src, dst_ref=dst, send_sem=send_sem, recv_sem=recv_sem,
            device_id=(tile, frame), device_id_type=MESH,
        )

    loads = [
        pltpu.make_async_copy(
            interp.at[0, pl.ds(h * 8, 8)], itp.at[pl.ds(h * 8, 8)], itp_sem.at[h]
        )
        for h in range(H)
    ]
    for load in loads:
        load.start()

    barrier = pltpu.get_barrier_semaphore()
    for i in range(1, NP):
        pl.semaphore_signal(barrier, inc=1, device_id=(plane_tile(i), f), device_id_type=MESH)
    for i in range(1, NZ):
        pl.semaphore_signal(barrier, inc=1, device_id=(column_tile(i), f), device_id_type=MESH)
    for i in range(1, NX):
        pl.semaphore_signal(barrier, inc=1, device_id=(t, lax.rem(f + i, NX)), device_id_type=MESH)

    values = dot(feats[0], w_value[...])
    values_t = values.T
    v_rows[0:256] = values_t[:, 0:128]
    v_rows[256:512] = values_t[:, 128:256]
    for half in range(2):
        def spread(e, _, half=half):
            d = half * 16 + e
            tiles = [v_rows[pl.ds(l * 256 + d, 8, stride=32), :] for l in range(2)]
            ag[half, 0:16, block(e, 128)] = jnp.concatenate(tiles, axis=0).astype(BF16)
            return 0
        lax.fori_loop(0, 16, spread, 0)

    pl.semaphore_wait(barrier, NP - 1 + NZ - 1 + NX - 1)

    def ring(side, s, half):
        if side == 0:
            src, dst, to = (NZ - s) % NZ, NZ - 1 - s, right
        else:
            src, dst, to = s, s + 1, left
        return remote(
            ag.at[half, pl.ds(src * 16, 16)], ag.at[half, pl.ds(dst * 16, 16)],
            ag_send_sem.at[side, s, half], ag_recv_sem.at[side, s, half], to, f,
        )

    ring_steps = [
        [(side, s, half) for half in range(2) for side in range(2) if s < 3 or half == side]
        for s in range(4)
    ]
    for step in ring_steps[0]:
        ring(*step).start()

    route_s[...] = jnp.full(route_s.shape, -1, jnp.int32)
    route_s[:, 0:64] = routes[0, block(z, NP), :]
    row = lax.broadcasted_iota(jnp.int32, (128, 128), 0)
    lane = lax.broadcasted_iota(jnp.int32, (128, 128), 1)
    row_rel = lax.rem(lax.div(row, 2), 8)
    row_slot = lax.rem(row, 2)
    row_plane = lax.div(row, 16)
    owner_z = lax.rem(z + row_rel, NZ) * NP

    def picks(named, owner):
        hit = named == owner
        first = jnp.min(jnp.where(hit, lane, 128), axis=1, keepdims=True)
        is_first = jnp.where(lane == first, 1, 0)
        return jnp.where(hit & (is_first == 1 - row_slot), 1.0, 0.0).astype(F32)

    mine_now = picks(jnp.broadcast_to(route_s[pl.ds(p, 1), :], (128, 128)), owner_z + row_plane)
    mine_t[...] = mine_now.astype(BF16)
    mine[...] = mine_now.T.astype(BF16)
    readers = jnp.broadcast_to(route_s[...][:, None, :], (8, 16, 128)).reshape(128, 128)
    asked = picks(readers, owner_z + p)
    piece_of = lax.rem(lax.div(row, 4), 2) * 8 + lax.div(row, 8)
    pieces = jnp.where(piece_of == lax.rem(lane, 16), 1.0, 0.0).astype(BF16)
    to_piece = dot(asked.astype(BF16), pieces)
    to_piece = jnp.where(row_rel == lax.div(lane, 16), to_piece, 0.0)
    pick_f[...] = to_piece.astype(BF16)
    pick_r[...] = to_piece.T.astype(BF16)

    logits = dot(w_attn_t[...], feats[0], NT).reshape(H, 8, 256)
    powers = jnp.exp(logits - jnp.max(logits, axis=1, keepdims=True))
    attn_s[...] = (powers / jnp.sum(powers, axis=1, keepdims=True)).reshape(64, 256)
    gm_s[...] = dot(w_out[...], grad_out[0], NT)
    feats_t[...] = feats[0].astype(F32).T.astype(BF16)

    for h in range(H):
        loads[h].wait()

    def contribute(h, _):
        grad_mixed = gm_s[block(h, 32), :]
        weights = attn_s[block(h, 8), :]
        for i in range(8):
            grad_sampled = (weights[i:i + 1] * grad_mixed).astype(BF16)
            con[block(h * 8 + i, 32), :] = dot(grad_sampled, itp[h * 8 + i])
        return 0
    lax.fori_loop(0, H, contribute, 0)

    def plane_copy(send, recv, send_sem, recv_sem, half, i):
        return remote(
            send.at[half, block(lax.rem(p + i, NP), 16)], recv.at[half, block(p, 16)],
            send_sem.at[half, i - 1], recv_sem.at[half, i - 1], plane_tile(i), f,
        )

    def plane_wait(recv, recv_sem, half, i):
        there = recv.at[half, block(lax.rem(p + NP - i, NP), 16)]
        pltpu.make_async_copy(there, there, recv_sem.at[half, i - 1]).wait()

    for half in range(2):
        def lay(e, _, half=half):
            d = half * 16 + e
            for g in range(4):
                tiles = [con[pl.ds((g * 2 + k) * 256 + d, 8, stride=32), :] for k in range(2)]
                con_rows[half, g * 16:(g + 1) * 16, block(e, 128)] = jnp.concatenate(tiles, axis=0).astype(BF16)
            return 0
        lax.fori_loop(0, 16, lay, 0)

        def choose(e, _, half=half):
            send_r[half, :, block(e, 512)] = dot(
                mine_t[:, 0:64], con_rows[half, :, block(e, 512)]
            ).astype(BF16)
            return 0
        lax.fori_loop(0, 4, choose, 0)
        for i in range(1, NP):
            plane_copy(send_r, recv_r, r_send_sem, r_recv_sem, half, i).start()
        recv_r[half, block(p, 16), :] = send_r[half, block(p, 16), :]

    for s in range(1, 4):
        for side, _, half in ring_steps[s - 1]:
            ring(side, s - 1, half).wait_recv()
            if (side, s, half) in ring_steps[s]:
                ring(side, s, half).start()
    for step in ring_steps[3]:
        ring(*step).wait_recv()

    for half in range(2):
        def answer(e, _, half=half):
            send_f[half, :, block(e, 512)] = dot(pick_f[...], ag[half, :, block(e, 512)]).astype(BF16)
            return 0
        lax.fori_loop(0, 4, answer, 0)
        for i in range(1, NP):
            plane_copy(send_f, recv_f, f_send_sem, f_recv_sem, half, i).start()
        recv_f[half, block(p, 16), :] = send_f[half, block(p, 16), :]

    def chain(side, s, half):
        return remote(
            rs_send.at[side, s, half], rs_recv.at[side, s, half],
            rs_send_sem.at[side, s, half], rs_recv_sem.at[side, s, half],
            right if side == 0 else left, f,
        )

    def chain_send(side, s, half):
        rel = 4 - s if side == 0 else 4 + s
        total = acc[half, rel * 16:(rel + 1) * 16, :]
        if s >= 1 and (side, s - 1, half) in chain_steps[s - 1]:
            chain(side, s - 1, half).wait_recv()
            total = total + rs_recv[side, s - 1, half].astype(F32)
        rs_send[side, s, half] = total.astype(BF16)
        chain(side, s, half).start()

    chain_steps = [
        [(side, s, half) for half in range(2) for side in range(2) if s > 0 or half == side]
        for s in range(4)
    ]
    for half in range(2):
        for i in range(1, NP):
            plane_wait(recv_r, r_recv_sem, half, i)
        def add_up(e, _, half=half):
            acc[half, :, block(e, 512)] = dot(pick_r[...], recv_r[half, :, block(e, 512)])
            return 0
        lax.fori_loop(0, 4, add_up, 0)
        chain_send(half, 0, half)
    for s in range(1, 4):
        for step in chain_steps[s]:
            chain_send(*step)

    for half in range(2):
        for i in range(1, NP):
            plane_wait(recv_f, f_recv_sem, half, i)
        def fetch(e, _, half=half):
            rows = dot(mine[0:64, :], recv_f[half, :, block(e, 512)])
            for k in range(4):
                d = half * 16 + e * 4 + k
                for g in range(8):
                    fet[pl.ds(g * 256 + d, 8, stride=32), :] = rows[g * 8:(g + 1) * 8, k * 128:(k + 1) * 128]
            return 0
        lax.fori_loop(0, 4, fetch, 0)

    def sample(h, _):
        grad_mixed = gm_s[block(h, 32), :]
        weights = attn_s[block(h, 8), :]
        mixed = jnp.zeros((32, 256), F32)
        grads = []
        for i in range(8):
            j = h * 8 + i
            sampled = dot(fet[block(j, 32), :].astype(BF16), itp[j], NT)
            mixed = mixed + weights[i:i + 1] * sampled
            grads.append(jnp.sum(grad_mixed * sampled, axis=0, keepdims=True))
        mixed_s[block(h, 32), :] = mixed.astype(BF16)
        ga_s[block(h, 8), :] = jnp.concatenate(grads, axis=0)
        return 0
    lax.fori_loop(0, H, sample, 0)

    attn = attn_s[...].reshape(H, 8, 256)
    grad_attn = ga_s[...].reshape(H, 8, 256)
    inner = jnp.sum(attn * grad_attn, axis=1, keepdims=True)
    grad_logits = (attn * (grad_attn - inner)).reshape(64, 256)
    part_attn = dot(grad_logits.astype(BF16), feats[0])
    part_out = dot(mixed_s[...], grad_out[0])
    grad_query = dot(grad_logits.T.astype(BF16), w_attn_t[...])

    for half in range(2):
        total = acc[half, 0:16, :]
        for side in range(2):
            chain(side, 3, half).wait_recv()
            total = total + rs_recv[side, 3, half].astype(F32)
        for e in range(16):
            for l in range(2):
                gv_rows[pl.ds(l * 256 + half * 16 + e, 8, stride=32), :] = total[l * 8:(l + 1) * 8, e * 128:(e + 1) * 128]
    grad_values = jnp.concatenate([gv_rows[0:256].T, gv_rows[256:512].T], axis=0).astype(BF16)
    part_value = dot(feats_t[...], grad_values)

    for q in range(NP):
        lanes = slice((q // 4) * 128, (q // 4 + 1) * 128)
        k = q % 4
        rp_send[q, 0:64] = part_value[k * 64:(k + 1) * 64, lanes].astype(BF16)
        rp_send[q, 64:128] = part_out[k * 64:(k + 1) * 64, lanes].astype(BF16)
        rp_send[q, 128:144] = part_attn[k * 16:(k + 1) * 16, lanes].astype(BF16)

    def share_copy(i):
        return remote(
            rp_send.at[lax.rem(p + i, NP)], rp_recv.at[i - 1],
            p_send_sem.at[i - 1], p_recv_sem.at[i - 1], plane_tile(i), f,
        )
    for i in range(1, NP):
        share_copy(i).start()
    grad_feats[0] = (grad_query + dot(grad_values, w_value[...], NT)).astype(BF16)
    total = rp_send[p].astype(F32)
    for i in range(1, NP):
        share_copy(i).wait_recv()
        total = total + rp_recv[i - 1].astype(F32)
    for q in range(NZ):
        rz_send[q, 0:8] = total[q * 8:(q + 1) * 8]
        rz_send[q, 8:16] = total[64 + q * 8:64 + (q + 1) * 8]
        rz_send[q, 16:32] = total[128:144]

    def column_copy(i):
        return remote(
            rz_send.at[lax.rem(z + i, NZ)], rz_recv.at[z],
            z_send_sem.at[i - 1], z_recv_sem.at[i - 1], column_tile(i), f,
        )
    for i in range(1, NZ):
        column_copy(i).start()
    rz_recv[z] = rz_send[z]
    for i in range(1, NZ):
        there = rz_recv.at[lax.rem(z + NZ - i, NZ)]
        pltpu.make_async_copy(there, there, z_recv_sem.at[i - 1]).wait()
    total = rz_recv[0]
    for q in range(1, NZ):
        total = total + rz_recv[q]
    rx_recv[f] = total

    def frame_copy(i):
        return remote(
            rx_recv.at[f], rx_recv.at[f],
            x_send_sem.at[i - 1], x_recv_sem.at[i - 1], t, lax.rem(f + i, NX),
        )
    for i in range(1, NX):
        frame_copy(i).start()
    for i in range(1, NX):
        there = rx_recv.at[lax.rem(f + NX - i, NX)]
        pltpu.make_async_copy(there, there, x_recv_sem.at[i - 1]).wait()
    total = rx_recv[0]
    for q in range(1, NX):
        total = total + rx_recv[q]
    gz[z] = total[0:16]

    def gather_column(i):
        return remote(
            gz.at[z], gz.at[z],
            gz_send_sem.at[i - 1], gz_recv_sem.at[i - 1], column_tile(i), f,
        )
    for i in range(1, NZ):
        gather_column(i).start()
    for i in range(1, NZ):
        there = gz.at[lax.rem(z + NZ - i, NZ)]
        pltpu.make_async_copy(there, there, gz_recv_sem.at[i - 1]).wait()
    gathered = [gz[q] for q in range(NZ)]
    gp[p] = jnp.concatenate(
        [g[0:8] for g in gathered] + [g[8:16] for g in gathered] + [total[16:32]], axis=0
    ).astype(BF16)

    def gather_plane(i):
        return remote(
            gp.at[p], gp.at[p],
            gp_send_sem.at[i - 1], gp_recv_sem.at[i - 1], plane_tile(i), f,
        )
    for i in range(1, NP):
        gather_plane(i).start()
    for i in range(1, NP):
        there = gp.at[lax.rem(p + NP - i, NP)]
        pltpu.make_async_copy(there, there, gp_recv_sem.at[i - 1]).wait()
    factor = 1.0 / math.sqrt(NX * NZ * NP * 256)
    for q in range(NP):
        lanes = slice((q // 4) * 128, (q // 4 + 1) * 128)
        k = q % 4
        grad_w_value[k * 64:(k + 1) * 64, lanes] = gp[q, 0:64].astype(F32) * factor
        grad_w_out[k * 64:(k + 1) * 64, lanes] = gp[q, 64:128].astype(F32) * factor
        grad_w_attn_t[k * 16:(k + 1) * 16, lanes] = gp[q, 128:144].astype(F32) * factor

    for steps in ring_steps:
        for step in steps:
            ring(*step).wait_send()
    for steps in chain_steps:
        for step in steps:
            chain(*step).wait_send()
    for half in range(2):
        for i in range(1, NP):
            plane_copy(send_f, recv_f, f_send_sem, f_recv_sem, half, i).wait_send()
            plane_copy(send_r, recv_r, r_send_sem, r_recv_sem, half, i).wait_send()
    for i in range(1, NP):
        share_copy(i).wait_send()
        gather_plane(i).wait_send()
    for i in range(1, NZ):
        column_copy(i).wait_send()
        gather_column(i).wait_send()
    for i in range(1, NX):
        frame_copy(i).wait_send()


def per_device(feats, routes, interp, w_value, w_attn, w_out, grad_out):
    vmem = pl.BlockSpec(memory_space=pltpu.VMEM)
    dma = pltpu.SemaphoreType.DMA
    outs = pl.pallas_call(
        kernel,
        out_shape=(
            jax.ShapeDtypeStruct((1, 256, 256), BF16),
            jax.ShapeDtypeStruct((256, 256), F32),
            jax.ShapeDtypeStruct((64, 256), F32),
            jax.ShapeDtypeStruct((256, 256), F32),
        ),
        in_specs=[vmem, vmem, pl.BlockSpec(memory_space=pl.ANY)] + [vmem] * 4,
        out_specs=(vmem,) * 4,
        scratch_shapes=[
            pltpu.VMEM((64, 256, 128), BF16),
            pltpu.VMEM((512, 128), F32),
            pltpu.VMEM((2, 128, HALF), BF16),
            pltpu.VMEM((2, 128, HALF), BF16),
            pltpu.VMEM((2, 128, HALF), BF16),
            pltpu.VMEM((2, 128, HALF), BF16),
            pltpu.VMEM((2, 128, HALF), BF16),
            pltpu.VMEM((2, 128, HALF), F32),
            pltpu.VMEM((2, 4, 2, 16, HALF), BF16),
            pltpu.VMEM((2, 4, 2, 16, HALF), BF16),
            pltpu.VMEM((2048, 128), F32),
            pltpu.VMEM((2, 64, HALF), BF16),
            pltpu.VMEM((2048, 128), F32),
            pltpu.VMEM((64, 256), F32),
            pltpu.VMEM((256, 256), F32),
            pltpu.VMEM((64, 256), F32),
            pltpu.VMEM((256, 256), BF16),
            pltpu.VMEM((256, 256), BF16),
            pltpu.VMEM((128, 128), BF16),
            pltpu.VMEM((128, 128), BF16),
            pltpu.VMEM((128, 128), BF16),
            pltpu.VMEM((128, 128), BF16),
            pltpu.VMEM((8, 128), jnp.int32),
            pltpu.VMEM((512, 128), F32),
            pltpu.VMEM((NP, SHARE, 128), BF16),
            pltpu.VMEM((NP - 1, SHARE, 128), BF16),
            pltpu.VMEM((SHARE, 128), F32),
            pltpu.VMEM((NZ, 32, 128), F32),
            pltpu.VMEM((NZ, 32, 128), F32),
            pltpu.VMEM((NX, 32, 128), F32),
            pltpu.VMEM((NZ, 16, 128), F32),
            pltpu.VMEM((NP, SHARE, 128), BF16),
            dma((H,)),
            pltpu.SemaphoreType.REGULAR,
            dma((2, 4, 2)),
            dma((2, 4, 2)),
            dma((2, NP - 1)),
            dma((2, NP - 1)),
            dma((2, NP - 1)),
            dma((2, NP - 1)),
            dma((2, 4, 2)),
            dma((2, 4, 2)),
            dma((NP - 1,)),
            dma((NP - 1,)),
            dma((NZ - 1,)),
            dma((NZ - 1,)),
            dma((NX - 1,)),
            dma((NX - 1,)),
            dma((NZ - 1,)),
            dma((NZ - 1,)),
            dma((NP - 1,)),
            dma((NP - 1,)),
        ],
        compiler_params=pltpu.CompilerParams(
            collective_id=0, has_side_effects=True, vmem_limit_bytes=48 * 1024 * 1024
        ),
    )(feats, routes, interp, w_value, w_attn.T, w_out, grad_out)
    return outs[0], outs[1], outs[2].T, outs[3]


def solution(mesh):
    in_specs = (
        P("frame", "tile", None),
        P("frame", None, None),
        P("frame", None, "tile", None),
        P(),
        P(),
        P(),
        P("frame", "tile", None),
    )
    out_specs = (P("frame", "tile", None), P(), P(), P())
    return jax.shard_map(
        per_device, mesh=mesh, in_specs=in_specs, out_specs=out_specs, check_vma=False
    )
```

```python
import math

import jax
import jax.numpy as jnp
from jax import lax
from jax.experimental import pallas as pl
from jax.experimental.pallas import tpu as pltpu
from jax.sharding import PartitionSpec as P

MESH = pl.DeviceIdType.MESH
F32 = jnp.float32
BF16 = jnp.bfloat16
NZ = 8
NP = 8
NX = 4
H = 8
SHARE = 144
PLACE = {0: 0, 1: 1, 7: 2, 2: 3, 6: 4, 3: 5, 5: 6, 4: 7}
GROUPS = ((0, 1), (1, 2), (3, 2), (5, 2), (7, 1))
NN = (((1,), (0,)), ((), ()))
NT = (((1,), (1,)), ((), ()))


def dot(a, b, dims=NN):
    return lax.dot_general(a, b, dims, preferred_element_type=F32)


def block(index, size):
    return pl.ds(pl.multiple_of(index * size, size), size)


def one_hot(hit):
    return jnp.where(hit, 1.0, 0.0).astype(BF16)


def kernel(
    feats_hbm, routes_hbm, interp, w_value_hbm, w_attn_hbm, w_out_hbm, grad_out_hbm,
    grad_feats, sums,
    feats, routes, w_value, w_attn_t, w_out, grad_out, itp, v_rows,
    ag, send_f, recv_f, send_r, recv_r, acc, rs_send, rs_recv,
    con, con_rows, fet, fetched, attn_s, gm_s, ga_s, mixed_s, feats_t,
    pick_f, pick_r, mine_t, mine, route_s, gv_rows,
    rp_send, rp_recv, rz_send, rz_recv, rx_recv, gz, gp,
    in_sem, itp_sem, ag_send_sem, ag_recv_sem, f_send_sem, f_recv_sem,
    r_send_sem, r_recv_sem, rs_send_sem, rs_recv_sem, sum_send_sem, sum_recv_sem,
):
    t = lax.axis_index("tile")
    f = lax.axis_index("frame")
    z = lax.div(t, NP)
    p = lax.rem(t, NP)

    def plane_tile(i):
        return z * NP + lax.rem(p + i, NP)

    def column_tile(i):
        return lax.rem(z + i, NZ) * NP + p

    right = column_tile(1)
    left = column_tile(NZ - 1)

    leaving, coming = [], {}

    def remote(src, dst, send_sem, recv_sem, tile, frame):
        return pltpu.make_async_remote_copy(
            src_ref=src, dst_ref=dst, send_sem=send_sem, recv_sem=recv_sem,
            device_id=(tile, frame), device_id_type=MESH,
        )

    def send(key, copy):
        copy.start()
        leaving.append(copy.wait_send)
        coming[key] = copy.wait_recv

    def send_many(key, copies, size, send_sem, recv_sem):
        for copy in copies:
            copy.start()
        leaving.append(pltpu.make_async_copy(size, size, send_sem).wait)
        coming[key] = pltpu.make_async_copy(size, size, recv_sem).wait

    def arrive(key):
        coming.pop(key)()

    def settle():
        for key in list(coming):
            arrive(key)
        for wait in leaving:
            wait()

    barrier = pltpu.get_barrier_semaphore()
    near = [(plane_tile(i), f) for i in range(1, NP)] + [(right, f), (left, f)]
    near += [(t, lax.rem(f + i, NX)) for i in range(1, NX)]
    for device in near:
        pl.semaphore_signal(barrier, inc=1, device_id=device, device_id_type=MESH)

    ins = [
        pltpu.make_async_copy(src, dst, in_sem.at[i])
        for i, (src, dst) in enumerate((
            (feats_hbm, feats), (w_value_hbm, w_value), (routes_hbm, routes),
            (w_attn_hbm, w_attn_t), (w_out_hbm, w_out), (grad_out_hbm, grad_out),
        ))
    ]
    loads = [
        pltpu.make_async_copy(
            interp.at[0, pl.ds(h * 8, 8)], itp.at[pl.ds(h * 8, 8)], itp_sem.at[h]
        )
        for h in range(H)
    ]
    for load in ins + loads:
        load.start()

    ins[0].wait()
    ins[1].wait()
    values_t = dot(feats[0], w_value[...]).T
    v_rows[0:256] = values_t[:, 0:128]
    v_rows[256:512] = values_t[:, 128:256]
    for k in range(0, 16, 2):
        for c in range(4):
            tiles = [v_rows[pl.ds((k + m) * 32 + c, 8, stride=4), :] for m in range(2)]
            ag[0, k * 8:(k + 2) * 8, c * 128:(c + 1) * 128] = jnp.concatenate(tiles, axis=0).astype(BF16)
    for load in ins[2:]:
        load.wait()

    route_s[...] = jnp.full(route_s.shape, -1, jnp.int32)
    route_s[:, 0:64] = routes[0, block(z, NP), :]
    row = lax.broadcasted_iota(jnp.int32, (128, 128), 0)
    lane = lax.broadcasted_iota(jnp.int32, (128, 128), 1)
    place = lax.div(row, 16)
    distance = jnp.where(lax.rem(place, 2) == 1, lax.div(place + 1, 2), NZ - lax.div(place, 2))
    row_slot = lax.rem(row, 2)
    row_plane = lax.rem(lax.div(row, 2), NP)
    owner_z = lax.rem(z + distance, NZ) * NP

    def picks(named, owner):
        hit = named == owner
        first = jnp.min(jnp.where(hit, lane, 128), axis=1, keepdims=True)
        is_first = jnp.where(lane == first, 1, 0)
        return jnp.where(hit & (is_first == 1 - row_slot), 1.0, 0.0).astype(F32)

    def same_row(shape):
        return lax.rem(lax.broadcasted_iota(jnp.int32, shape, 0), 8) == lax.rem(
            lax.broadcasted_iota(jnp.int32, shape, 1), 8
        )

    def by_eight(x):
        return jnp.broadcast_to(x[:, None, :], (x.shape[0], 8, x.shape[1])).reshape(x.shape[0] * 8, x.shape[1])

    def eighth(shape):
        return one_hot(
            lax.div(lax.broadcasted_iota(jnp.int32, shape, 1), 8) == lax.broadcasted_iota(jnp.int32, shape, 0)
        )

    mine_now = picks(jnp.broadcast_to(route_s[pl.ds(p, 1), :], (128, 128)), owner_z + row_plane)
    mine_wide = dot(mine_now.astype(BF16), eighth((128, 512)))
    mine_wide_t = dot(mine_now.T[0:64].astype(BF16), eighth((128, 1024)))
    readers = jnp.broadcast_to(
        jnp.broadcast_to(route_s[...][:, None, :], (8, 2, 128)).reshape(16, 128)[None], (8, 16, 128)
    ).reshape(128, 128)
    asked = picks(readers, owner_z + p)
    piece_of = lax.rem(lax.div(row, 4), 2) * 8 + lax.div(row, 8)
    to_piece = dot(asked.astype(BF16), one_hot(piece_of == lax.div(lane, 8)))
    keep = same_row((128, 128))
    keep_wide = same_row((128, 512))
    keep_long = same_row((512, 128))
    for q in range(8):
        mine_t[q] = jnp.where(keep_wide, by_eight(mine_wide[q * 16:(q + 1) * 16]), 0.0).astype(BF16)
        mine[:, q * 128:(q + 1) * 128] = jnp.where(
            keep_long, by_eight(mine_wide_t[:, q * 128:(q + 1) * 128]), 0.0
        ).astype(BF16)
        piece = jnp.where(keep, by_eight(to_piece[q * 16:(q + 1) * 16]), 0.0)
        pick_f[q] = piece.astype(BF16)
        pick_r[q] = piece.T.astype(BF16)

    logits = dot(w_attn_t[...], feats[0], NT).reshape(H, 8, 256)
    powers = jnp.exp(logits - jnp.max(logits, axis=1, keepdims=True))
    attn_s[...] = (powers / jnp.sum(powers, axis=1, keepdims=True)).reshape(64, 256)
    gm_s[...] = dot(w_out[...], grad_out[0], NT)

    for load in loads:
        load.wait()

    def contribute(h, _):
        grad_mixed = gm_s[block(h, 32), :]
        weights = attn_s[block(h, 8), :]
        for i in range(8):
            grad_sampled = (weights[i:i + 1] * grad_mixed).astype(BF16)
            con[i * 32:(i + 1) * 32, :] = dot(grad_sampled, itp[h * 8 + i])
        for i in range(0, 8, 2):
            for c in range(4):
                tiles = [con[pl.ds((i + m) * 32 + c, 8, stride=4), :] for m in range(2)]
                con_rows[block(h * 4 + i // 2, 16), c * 128:(c + 1) * 128] = jnp.concatenate(tiles, axis=0).astype(BF16)
        return 0
    lax.fori_loop(0, H, contribute, 0)

    def choose(q, _):
        send_r[q] = dot(mine_t[q], con_rows[...]).astype(BF16)
        return 0
    lax.fori_loop(0, 8, choose, 0)

    def answer(q):
        send_f[q] = dot(pick_f[q], ag[q]).astype(BF16)
    answer(0)

    pl.semaphore_wait(barrier, len(near))

    def ring(side, s, half):
        if side == 0:
            src, dst, to = (NZ - s) % NZ, NZ - 1 - s, right
        else:
            src, dst, to = s, s + 1, left
        rows = pl.ds(half * 64, 64)
        return remote(
            ag.at[PLACE[src], rows], ag.at[PLACE[dst], rows],
            ag_send_sem.at[side, s, half], ag_recv_sem.at[side, s, half], to, f,
        )

    ring_steps = [
        [(side, s, half) for order in range(2) for side in range(2)
         for half in ((side + order) % 2,) if s < 3 or half == side]
        for s in range(4)
    ]
    for step in ring_steps[0]:
        send(("ring", *step), ring(*step))

    def plane_send(name, src, dst, send_sem, recv_sem, g):
        first, count = GROUPS[g]
        blocks = pl.ds(first, count)
        copies = [
            remote(
                src.at[blocks, block(lax.rem(p + i, NP), 16)], dst.at[blocks, block(p, 16)],
                send_sem.at[g], recv_sem.at[g], plane_tile(i), f,
            )
            for i in range(1, NP)
        ]
        send_many((name, g), copies, dst.at[blocks, pl.ds(0, 16 * (NP - 1))], send_sem.at[g], recv_sem.at[g])
        for q in range(first, first + count):
            dst[q, block(p, 16), :] = src[q, block(p, 16), :]

    for g in (4, 3, 2, 1, 0):
        plane_send("r", send_r, recv_r, r_send_sem, r_recv_sem, g)
    plane_send("f", send_f, recv_f, f_send_sem, f_recv_sem, 0)
    feats_t[...] = feats[0].astype(F32).T.astype(BF16)

    def chain(side, s, half):
        rows = pl.ds(half * 64, 64)
        return remote(
            rs_send.at[side, s, rows], rs_recv.at[side, s, rows],
            rs_send_sem.at[side, s, half], rs_recv_sem.at[side, s, half],
            right if side == 0 else left, f,
        )

    def add_up(g):
        arrive(("r", g))
        for q in range(GROUPS[g][0], GROUPS[g][0] + GROUPS[g][1]):
            acc[q] = dot(pick_r[q], recv_r[q])

    def chain_send(side, s, half):
        rows = slice(half * 64, half * 64 + 64)
        total = acc[PLACE[4 - s if side == 0 else 4 + s], rows]
        if s > 1 or (s == 1 and half == side):
            arrive(("chain", side, s - 1, half))
            total = total + rs_recv[side, s - 1, rows].astype(F32)
        rs_send[side, s, rows] = total.astype(BF16)
        send(("chain", side, s, half), chain(side, s, half))

    add_up(4)
    for side in range(2):
        chain_send(side, 0, side)
    for s in range(1, 4):
        for side, _, half in ring_steps[s - 1]:
            arrive(("ring", side, s - 1, half))
            if (side, s, half) in ring_steps[s]:
                send(("ring", side, s, half), ring(side, s, half))
        for q in range(GROUPS[s][0], GROUPS[s][0] + 2):
            answer(q)
        plane_send("f", send_f, recv_f, f_send_sem, f_recv_sem, s)
        add_up(4 - s)
        for order in range(2):
            for side in range(2):
                chain_send(side, s, (1 - side + order) % 2)
    for step in ring_steps[3]:
        arrive(("ring", *step))
    answer(7)
    plane_send("f", send_f, recv_f, f_send_sem, f_recv_sem, 4)
    add_up(0)

    total = acc[0]
    for side in range(2):
        for half in range(2):
            arrive(("chain", side, 3, half))
        total = total + rs_recv[side, 3].astype(F32)
    for k in range(16):
        for c in range(4):
            gv_rows[pl.ds(k * 32 + c, 8, stride=4), :] = total[k * 8:(k + 1) * 8, c * 128:(c + 1) * 128]
    grad_values = jnp.concatenate([gv_rows[0:256].T, gv_rows[256:512].T], axis=0).astype(BF16)
    part_value = dot(feats_t[...], grad_values)
    gm_value = dot(grad_values, w_value[...], NT)

    for g in range(4):
        arrive(("f", g))
    near_rows = recv_f[0:7].reshape(7 * 128, 512)

    def fetch(e, _):
        fetched[block(e, 128), :] = dot(mine[block(e, 128), 0:896], near_rows)
        return 0
    lax.fori_loop(0, 4, fetch, 0)
    arrive(("f", 4))

    def sample(h, _):
        grad_mixed = gm_s[block(h, 32), :]
        weights = attn_s[block(h, 8), :]
        maps = fetched[block(h, 64), :] + dot(mine[block(h, 64), 896:1024], recv_f[7])
        for i in range(8):
            for c in range(4):
                fet[pl.ds(i * 32 + c, 8, stride=4), :] = maps[i * 8:(i + 1) * 8, c * 128:(c + 1) * 128]
        mixed = jnp.zeros((32, 256), F32)
        grads = []
        for i in range(8):
            sampled = dot(fet[i * 32:(i + 1) * 32, :].astype(BF16), itp[h * 8 + i], NT)
            mixed = mixed + weights[i:i + 1] * sampled
            grads.append(jnp.sum(grad_mixed * sampled, axis=0, keepdims=True))
        mixed_s[block(h, 32), :] = mixed.astype(BF16)
        ga_s[block(h, 8), :] = jnp.concatenate(grads, axis=0)
        return 0
    lax.fori_loop(0, H, sample, 0)

    attn = attn_s[...].reshape(H, 8, 256)
    grad_attn = ga_s[...].reshape(H, 8, 256)
    inner = jnp.sum(attn * grad_attn, axis=1, keepdims=True)
    grad_logits = (attn * (grad_attn - inner)).reshape(64, 256)
    part_attn = dot(grad_logits.astype(BF16), feats[0])
    part_out = dot(mixed_s[...], grad_out[0])

    for q in range(NP):
        lanes = slice((q // 4) * 128, (q // 4 + 1) * 128)
        k = q % 4
        rp_send[q, 0:64] = part_value[k * 64:(k + 1) * 64, lanes].astype(BF16)
        rp_send[q, 64:128] = part_out[k * 64:(k + 1) * 64, lanes].astype(BF16)
        rp_send[q, 128:144] = part_attn[k * 16:(k + 1) * 16, lanes].astype(BF16)

    def exchange(stage, count, src, dst, device):
        send_sem, recv_sem = sum_send_sem.at[stage], sum_recv_sem.at[stage]
        copies = [remote(src(i), dst[1], send_sem, recv_sem, *device(i)) for i in range(1, count)]
        send_many(stage, copies, dst[0].at[pl.ds(0, count - 1)], send_sem, recv_sem)

    exchange(
        0, NP, lambda i: rp_send.at[lax.rem(p + i, NP)], (rp_recv, rp_recv.at[p]), lambda i: (plane_tile(i), f)
    )
    rp_recv[p] = rp_send[p]
    grad_query = dot(grad_logits.T.astype(BF16), w_attn_t[...])
    grad_feats[0] = (grad_query + gm_value).astype(BF16)
    arrive(0)
    total = rp_recv[0].astype(F32)
    for q in range(1, NP):
        total = total + rp_recv[q].astype(F32)
    for q in range(NZ):
        rows = [total[q * 8:(q + 1) * 8], total[64 + q * 8:64 + (q + 1) * 8], total[128:144]]
        rz_send[q] = jnp.concatenate(rows, axis=0).astype(BF16)
    exchange(
        1, NZ, lambda i: rz_send.at[lax.rem(z + i, NZ)], (rz_recv, rz_recv.at[z]), lambda i: (column_tile(i), f)
    )
    rz_recv[z] = rz_send[z]
    arrive(1)
    total = rz_recv[0].astype(F32)
    for q in range(1, NZ):
        total = total + rz_recv[q].astype(F32)
    rx_recv[f] = total.astype(BF16)
    exchange(
        2, NX, lambda i: rx_recv.at[f], (rx_recv, rx_recv.at[f]), lambda i: (t, lax.rem(f + i, NX))
    )
    arrive(2)
    total = rx_recv[0].astype(F32)
    for q in range(1, NX):
        total = total + rx_recv[q].astype(F32)
    gz[z] = total[0:16].astype(BF16)
    exchange(3, NZ, lambda i: gz.at[z], (gz, gz.at[z]), lambda i: (column_tile(i), f))
    arrive(3)
    gathered = [gz[q].astype(F32) for q in range(NZ)]
    gp[p] = jnp.concatenate(
        [g[0:8] for g in gathered] + [g[8:16] for g in gathered] + [total[16:32]], axis=0
    ).astype(BF16)
    exchange(4, NP, lambda i: gp.at[p], (gp, gp.at[p]), lambda i: (plane_tile(i), f))
    arrive(4)
    sums[...] = gp[...]

    settle()


def finish(grad_in, sums, grad_feats, grad_w_value, grad_w_attn_t, grad_w_out):
    factor = 1.0 / math.sqrt(NX * NZ * NP * 256)
    grad_feats[...] = grad_in[...]
    for q in range(NP):
        lanes = slice((q // 4) * 128, (q // 4 + 1) * 128)
        k = q % 4
        grad_w_value[k * 64:(k + 1) * 64, lanes] = sums[q, 0:64].astype(F32) * factor
        grad_w_out[k * 64:(k + 1) * 64, lanes] = sums[q, 64:128].astype(F32) * factor
        grad_w_attn_t[k * 16:(k + 1) * 16, lanes] = sums[q, 128:144].astype(F32) * factor


def per_device(feats, routes, interp, w_value, w_attn, w_out, grad_out):
    vmem = pl.BlockSpec(memory_space=pltpu.VMEM)
    dma = pltpu.SemaphoreType.DMA
    moved, sums = pl.pallas_call(
        kernel,
        out_shape=(
            jax.ShapeDtypeStruct((1, 256, 256), BF16),
            jax.ShapeDtypeStruct((NP, SHARE, 128), BF16),
        ),
        in_specs=[pl.BlockSpec(memory_space=pltpu.HBM)] * 7,
        out_specs=(vmem,) * 2,
        scratch_shapes=[
            pltpu.VMEM((1, 256, 256), BF16),
            pltpu.VMEM((1, 64, 64), jnp.int32),
            pltpu.VMEM((256, 256), BF16),
            pltpu.VMEM((64, 256), BF16),
            pltpu.VMEM((256, 256), BF16),
            pltpu.VMEM((1, 256, 256), BF16),
            pltpu.VMEM((64, 256, 128), BF16),
            pltpu.VMEM((512, 128), F32),
            pltpu.VMEM((8, 128, 512), BF16),
            pltpu.VMEM((8, 128, 512), BF16),
            pltpu.VMEM((8, 128, 512), BF16),
            pltpu.VMEM((8, 128, 512), BF16),
            pltpu.VMEM((8, 128, 512), BF16),
            pltpu.VMEM((8, 128, 512), F32),
            pltpu.VMEM((2, 4, 128, 512), BF16),
            pltpu.VMEM((2, 4, 128, 512), BF16),
            pltpu.VMEM((256, 128), F32),
            pltpu.VMEM((512, 512), BF16),
            pltpu.VMEM((256, 128), F32),
            pltpu.VMEM((512, 512), F32),
            pltpu.VMEM((64, 256), F32),
            pltpu.VMEM((256, 256), F32),
            pltpu.VMEM((64, 256), F32),
            pltpu.VMEM((256, 256), BF16),
            pltpu.VMEM((256, 256), BF16),
            pltpu.VMEM((8, 128, 128), BF16),
            pltpu.VMEM((8, 128, 128), BF16),
            pltpu.VMEM((8, 128, 512), BF16),
            pltpu.VMEM((512, 1024), BF16),
            pltpu.VMEM((8, 128), jnp.int32),
            pltpu.VMEM((512, 128), F32),
            pltpu.VMEM((NP, SHARE, 128), BF16),
            pltpu.VMEM((NP, SHARE, 128), BF16),
            pltpu.VMEM((NZ, 32, 128), BF16),
            pltpu.VMEM((NZ, 32, 128), BF16),
            pltpu.VMEM((NX, 32, 128), BF16),
            pltpu.VMEM((NZ, 16, 128), BF16),
            pltpu.VMEM((NP, SHARE, 128), BF16),
            dma((6,)),
            dma((H,)),
            dma((2, 4, 2)),
            dma((2, 4, 2)),
            dma((5,)),
            dma((5,)),
            dma((5,)),
            dma((5,)),
            dma((2, 4, 2)),
            dma((2, 4, 2)),
            dma((5,)),
            dma((5,)),
        ],
        compiler_params=pltpu.CompilerParams(
            collective_id=0, has_side_effects=True, vmem_limit_bytes=63 * 1024 * 1024
        ),
    )(feats, routes, interp, w_value, w_attn.T, w_out, grad_out)
    grads = pl.pallas_call(
        finish,
        out_shape=(
            jax.ShapeDtypeStruct((1, 256, 256), BF16),
            jax.ShapeDtypeStruct((256, 256), F32),
            jax.ShapeDtypeStruct((64, 256), F32),
            jax.ShapeDtypeStruct((256, 256), F32),
        ),
        in_specs=[vmem] * 2,
        out_specs=(vmem,) * 4,
    )(moved, sums)
    return grads[0], grads[1], grads[2].T, grads[3]


def solution(mesh):
    in_specs = (
        P("frame", "tile", None),
        P("frame", None, None),
        P("frame", None, "tile", None),
        P(),
        P(),
        P(),
        P("frame", "tile", None),
    )
    out_specs = (P("frame", "tile", None), P(), P(), P())
    return jax.shard_map(
        per_device, mesh=mesh, in_specs=in_specs, out_specs=out_specs, check_vma=False
    )
```

```python
import math

import jax
import jax.numpy as jnp
from jax import lax
from jax.experimental import pallas as pl
from jax.experimental.pallas import tpu as pltpu
from jax.sharding import PartitionSpec as P

MESH = pl.DeviceIdType.MESH
F32 = jnp.float32
BF16 = jnp.bfloat16
NZ = 8
NP = 8
NX = 4
H = 8
SHARES = (64, 80)
PLACE = {0: 0, 1: 1, 7: 2, 2: 3, 6: 4, 3: 5, 5: 6, 4: 7}
GROUPS = ((0, 1), (1, 2), (3, 2), (5, 2), (7, 1))
NN = (((1,), (0,)), ((), ()))
NT = (((1,), (1,)), ((), ()))


def dot(a, b, dims=NN):
    return lax.dot_general(a, b, dims, preferred_element_type=F32)


def block(index, size):
    return pl.ds(pl.multiple_of(index * size, size), size)


def one_hot(hit):
    return jnp.where(hit, 1.0, 0.0).astype(BF16)


def kernel(
    feats_hbm, routes_hbm, interp, w_value_hbm, w_attn_hbm, w_out_hbm, grad_out_hbm,
    grad_feats, value_sums, other_sums,
    column_feats, routes, w_value, w_attn_t, w_out, grad_out, itp, v_rows,
    maps, send_f, recv_f, send_r, recv_r, acc, rs_send, rs_recv,
    con, con_rows, fet, fetched, attn_s, gm_s, ga_s, mixed_s, w_value_t, value_s,
    pick_f, pick_r, mine_t, mine, route_s, gv_rows,
    value_plane, value_in, value_x, value_z, value_all,
    other_plane, other_in, other_x, other_z, other_all,
    in_sem, itp_sem, ag_send_sem, ag_recv_sem, f_send_sem, f_recv_sem,
    r_send_sem, r_recv_sem, rs_send_sem, rs_recv_sem, sum_send_sem, sum_recv_sem,
):
    t = lax.axis_index("tile")
    f = lax.axis_index("frame")
    z = lax.div(t, NP)
    p = lax.rem(t, NP)

    def plane_tile(i):
        return z * NP + lax.rem(p + i, NP)

    def column_tile(i):
        return lax.rem(z + i, NZ) * NP + p

    right = column_tile(1)
    left = column_tile(NZ - 1)

    leaving, coming = [], {}

    def remote(src, dst, send_sem, recv_sem, tile, frame):
        return pltpu.make_async_remote_copy(
            src_ref=src, dst_ref=dst, send_sem=send_sem, recv_sem=recv_sem,
            device_id=(tile, frame), device_id_type=MESH,
        )

    def send(key, copy):
        copy.start()
        leaving.append(copy.wait_send)
        coming[key] = copy.wait_recv

    def send_many(key, copies, size, send_sem, recv_sem):
        for copy in copies:
            copy.start()
        leaving.append(pltpu.make_async_copy(size, size, send_sem).wait)
        coming[key] = pltpu.make_async_copy(size, size, recv_sem).wait

    def arrive(key):
        coming.pop(key)()

    def settle():
        for key in list(coming):
            arrive(key)
        for wait in leaving:
            wait()

    barrier = pltpu.get_barrier_semaphore()
    near = [(plane_tile(i), f) for i in range(1, NP)] + [(right, f), (left, f)]
    near += [(t, lax.rem(f + i, NX)) for i in range(1, NX)]
    for device in near:
        pl.semaphore_signal(barrier, inc=1, device_id=device, device_id_type=MESH)

    ins = [
        pltpu.make_async_copy(src, dst, in_sem.at[i])
        for i, (src, dst) in enumerate((
            (feats_hbm.at[0], column_feats.at[0]), (w_value_hbm, w_value), (routes_hbm, routes),
            (w_attn_hbm, w_attn_t), (w_out_hbm, w_out), (grad_out_hbm, grad_out),
        ))
    ]
    loads = [
        pltpu.make_async_copy(
            interp.at[0, pl.ds(h * 8, 8)], itp.at[pl.ds(h * 8, 8)], itp_sem.at[h]
        )
        for h in range(H)
    ]
    for load in ins + loads:
        load.start()

    def value_maps(q):
        for l in range(2):
            v_rows[l] = dot(w_value_t[...], column_feats[q, l * 128:(l + 1) * 128, :], NT)
            for h in range(0, 8, 2):
                for c in range(4):
                    tiles = [v_rows[l, pl.ds((h + m) * 32 + c, 8, stride=4), :] for m in range(2)]
                    rows = slice(l * 64 + h * 8, l * 64 + h * 8 + 16)
                    maps[q, rows, c * 128:(c + 1) * 128] = jnp.concatenate(tiles, axis=0).astype(BF16)

    ins[0].wait()
    ins[1].wait()
    w_value_t[...] = w_value[...].astype(F32).T.astype(BF16)
    value_maps(0)
    for load in ins[2:]:
        load.wait()

    route_s[...] = jnp.full(route_s.shape, -1, jnp.int32)
    route_s[:, 0:64] = routes[0, block(z, NP), :]
    row = lax.broadcasted_iota(jnp.int32, (128, 128), 0)
    lane = lax.broadcasted_iota(jnp.int32, (128, 128), 1)
    place = lax.div(row, 16)
    distance = jnp.where(lax.rem(place, 2) == 1, lax.div(place + 1, 2), NZ - lax.div(place, 2))
    row_slot = lax.rem(row, 2)
    row_plane = lax.rem(lax.div(row, 2), NP)
    owner_z = lax.rem(z + distance, NZ) * NP

    def picks(named, owner):
        hit = named == owner
        first = jnp.min(jnp.where(hit, lane, 128), axis=1, keepdims=True)
        is_first = jnp.where(lane == first, 1, 0)
        return jnp.where(hit & (is_first == 1 - row_slot), 1.0, 0.0).astype(F32)

    def same_row(shape):
        return lax.rem(lax.broadcasted_iota(jnp.int32, shape, 0), 8) == lax.rem(
            lax.broadcasted_iota(jnp.int32, shape, 1), 8
        )

    def by_eight(x):
        return jnp.broadcast_to(x[:, None, :], (x.shape[0], 8, x.shape[1])).reshape(x.shape[0] * 8, x.shape[1])

    def eighth(shape):
        return one_hot(
            lax.div(lax.broadcasted_iota(jnp.int32, shape, 1), 8) == lax.broadcasted_iota(jnp.int32, shape, 0)
        )

    mine_now = picks(jnp.broadcast_to(route_s[pl.ds(p, 1), :], (128, 128)), owner_z + row_plane)
    mine_wide = dot(mine_now.astype(BF16), eighth((128, 512)))
    mine_wide_t = dot(mine_now.T[0:64].astype(BF16), eighth((128, 1024)))
    readers = jnp.broadcast_to(
        jnp.broadcast_to(route_s[...][:, None, :], (8, 2, 128)).reshape(16, 128)[None], (8, 16, 128)
    ).reshape(128, 128)
    asked = picks(readers, owner_z + p)
    piece_of = lax.rem(lax.div(row, 4), 2) * 8 + lax.div(row, 8)
    to_piece = dot(asked.astype(BF16), one_hot(piece_of == lax.div(lane, 8)))
    keep = same_row((128, 128))
    keep_wide = same_row((128, 512))
    keep_long = same_row((512, 128))
    for q in range(8):
        mine_t[q] = jnp.where(keep_wide, by_eight(mine_wide[q * 16:(q + 1) * 16]), 0.0).astype(BF16)
        mine[:, q * 128:(q + 1) * 128] = jnp.where(
            keep_long, by_eight(mine_wide_t[:, q * 128:(q + 1) * 128]), 0.0
        ).astype(BF16)
        piece = jnp.where(keep, by_eight(to_piece[q * 16:(q + 1) * 16]), 0.0)
        pick_f[q] = piece.astype(BF16)
        pick_r[q] = piece.T.astype(BF16)

    logits = dot(w_attn_t[...], column_feats[0], NT).reshape(H, 8, 256)
    powers = jnp.exp(logits - jnp.max(logits, axis=1, keepdims=True))
    attn_s[...] = (powers / jnp.sum(powers, axis=1, keepdims=True)).reshape(64, 256)
    gm_s[...] = dot(w_out[...], grad_out[0], NT)

    for load in loads:
        load.wait()

    def contribute(h, _):
        grad_mixed = gm_s[block(h, 32), :]
        weights = attn_s[block(h, 8), :]
        for i in range(8):
            grad_sampled = (weights[i:i + 1] * grad_mixed).astype(BF16)
            con[i * 32:(i + 1) * 32, :] = dot(grad_sampled, itp[h * 8 + i])
        for i in range(0, 8, 2):
            for c in range(4):
                tiles = [con[pl.ds((i + m) * 32 + c, 8, stride=4), :] for m in range(2)]
                con_rows[block(h * 4 + i // 2, 16), c * 128:(c + 1) * 128] = jnp.concatenate(tiles, axis=0).astype(BF16)
        return 0
    lax.fori_loop(0, H, contribute, 0)

    def choose(q, _):
        send_r[q] = dot(mine_t[q], con_rows[...]).astype(BF16)
        return 0
    lax.fori_loop(0, 8, choose, 0)

    def answer(q):
        send_f[q] = dot(pick_f[q], maps[q]).astype(BF16)
    answer(0)

    pl.semaphore_wait(barrier, len(near))

    def ring(side, s, half):
        if side == 0:
            src, dst, to = (NZ - s) % NZ, NZ - 1 - s, right
        else:
            src, dst, to = s, s + 1, left
        rows = pl.ds(half * 128, 128)
        return remote(
            column_feats.at[PLACE[src], rows], column_feats.at[PLACE[dst], rows],
            ag_send_sem.at[side, s, half], ag_recv_sem.at[side, s, half], to, f,
        )

    ring_steps = [
        [(side, s, half) for order in range(2) for side in range(2)
         for half in ((side + order) % 2,) if s < 3 or half == side]
        for s in range(4)
    ]
    for step in ring_steps[0]:
        send(("ring", *step), ring(*step))

    def plane_send(name, src, dst, send_sem, recv_sem, g):
        first, count = GROUPS[g]
        blocks = pl.ds(first, count)
        copies = [
            remote(
                src.at[blocks, block(lax.rem(p + i, NP), 16)], dst.at[blocks, block(p, 16)],
                send_sem.at[g], recv_sem.at[g], plane_tile(i), f,
            )
            for i in range(1, NP)
        ]
        send_many((name, g), copies, dst.at[blocks, pl.ds(0, 16 * (NP - 1))], send_sem.at[g], recv_sem.at[g])
        for q in range(first, first + count):
            dst[q, block(p, 16), :] = src[q, block(p, 16), :]

    plane_send("f", send_f, recv_f, f_send_sem, f_recv_sem, 0)
    for g in range(3):
        plane_send("r", send_r, recv_r, r_send_sem, r_recv_sem, g)

    def chain(side, s, half):
        rows = pl.ds(half * 64, 64)
        return remote(
            rs_send.at[side, s, rows], rs_recv.at[side, s, rows],
            rs_send_sem.at[side, s, half], rs_recv_sem.at[side, s, half],
            right if side == 0 else left, f,
        )

    def lay_rows(total):
        for k in range(16):
            for c in range(4):
                gv_rows[pl.ds(k * 32 + c, 8, stride=4), :] = total[k * 8:(k + 1) * 8, c * 128:(c + 1) * 128]

    def add_up(g):
        arrive(("r", g))
        for q in range(GROUPS[g][0], GROUPS[g][0] + GROUPS[g][1]):
            total = dot(pick_r[q], recv_r[q])
            acc[q] = total
            lay_rows(total)
            part = dot(gv_rows[0:256].astype(BF16), column_feats[q, 0:128, :])
            part = part + dot(gv_rows[256:512].astype(BF16), column_feats[q, 128:256, :])
            value_s[...] = part if q == 0 else value_s[...] + part

    def chain_send(side, s, half):
        rows = slice(half * 64, half * 64 + 64)
        total = acc[PLACE[4 - s if side == 0 else 4 + s], rows]
        if s > 1 or (s == 1 and half == side):
            arrive(("chain", side, s - 1, half))
            total = total + rs_recv[side, s - 1, rows].astype(F32)
        rs_send[side, s, rows] = total.astype(BF16)
        send(("chain", side, s, half), chain(side, s, half))

    def chain_step(s):
        for order in range(2):
            for side in range(2):
                half = (1 - side + order) % 2
                if s > 0 or half == side:
                    chain_send(side, s, half)

    for s in range(1, 4):
        for side, _, half in ring_steps[s - 1]:
            arrive(("ring", side, s - 1, half))
            if (side, s, half) in ring_steps[s]:
                send(("ring", side, s, half), ring(side, s, half))
        for q in range(GROUPS[s][0], GROUPS[s][0] + 2):
            value_maps(q)
            answer(q)
        plane_send("f", send_f, recv_f, f_send_sem, f_recv_sem, s)
        if s < 3:
            plane_send("r", send_r, recv_r, r_send_sem, r_recv_sem, s + 2)
        add_up(s - 1)
    for step in ring_steps[3]:
        arrive(("ring", *step))
    value_maps(7)
    answer(7)
    plane_send("f", send_f, recv_f, f_send_sem, f_recv_sem, 4)
    add_up(4)
    chain_step(0)
    add_up(3)
    part_value = value_s[...].T

    def exchange(key, count, src, dst, here, device):
        send_sem, recv_sem = sum_send_sem.at[key], sum_recv_sem.at[key]
        copies = [remote(src(i), dst.at[here], send_sem, recv_sem, *device(i)) for i in range(1, count)]
        send_many(key, copies, dst.at[pl.ds(0, count - 1)], send_sem, recv_sem)

    def added(ref, count):
        total = ref[0].astype(F32)
        for q in range(1, count):
            total = total + ref[q].astype(F32)
        return total.astype(BF16)

    stages = (
        (value_plane, value_in, value_x, value_z, value_all),
        (other_plane, other_in, other_x, other_z, other_all),
    )

    def share_out(n):
        plane, inward = stages[n][0:2]
        exchange(
            n * 4, NP, lambda i: plane.at[lax.rem(p + i, NP)], inward, p, lambda i: (plane_tile(i), f)
        )
        inward[p] = plane[p]

    def along_x(n):
        arrive(n * 4)
        across = stages[n][2]
        across[f] = added(stages[n][1], NP)
        exchange(n * 4 + 1, NX, lambda i: across.at[f], across, f, lambda i: (t, lax.rem(f + i, NX)))

    def along_z(n):
        arrive(n * 4 + 1)
        up = stages[n][3]
        up[z] = added(stages[n][2], NX)
        exchange(n * 4 + 2, NZ, lambda i: up.at[z], up, z, lambda i: (column_tile(i), f))

    def share_back(n):
        arrive(n * 4 + 2)
        back = stages[n][4]
        back[p] = added(stages[n][3], NZ)
        exchange(n * 4 + 3, NP, lambda i: back.at[p], back, p, lambda i: (plane_tile(i), f))

    for q in range(NP):
        lanes = slice((q // 4) * 128, (q // 4 + 1) * 128)
        k = q % 4
        value_plane[q] = part_value[k * 64:(k + 1) * 64, lanes].astype(BF16)
    share_out(0)

    for g in range(4):
        arrive(("f", g))
    near_rows = recv_f[0:7].reshape(7 * 128, 512)

    def fetch(e, _):
        fetched[block(e, 128), :] = dot(mine[block(e, 128), 0:896], near_rows)
        return 0
    lax.fori_loop(0, 4, fetch, 0)
    arrive(("f", 4))

    def sample(e, _):
        rows = fetched[block(e, 128), :] + dot(mine[block(e, 128), 896:1024], recv_f[7])
        for i in range(16):
            for c in range(4):
                fet[pl.ds(i * 32 + c, 8, stride=4), :] = rows[i * 8:(i + 1) * 8, c * 128:(c + 1) * 128]
        for m in range(2):
            h = e * 2 + m
            grad_mixed = gm_s[block(h, 32), :]
            weights = attn_s[block(h, 8), :]
            mixed = jnp.zeros((32, 256), F32)
            grads = []
            for i in range(8):
                k = m * 8 + i
                sampled = dot(fet[k * 32:(k + 1) * 32, :].astype(BF16), itp[h * 8 + i], NT)
                mixed = mixed + weights[i:i + 1] * sampled
                grads.append(jnp.sum(grad_mixed * sampled, axis=0, keepdims=True))
            mixed_s[block(h, 32), :] = mixed.astype(BF16)
            ga_s[block(h, 8), :] = jnp.concatenate(grads, axis=0)
        return 0
    lax.fori_loop(0, 2, sample, 0)
    along_x(0)
    chain_step(1)
    lax.fori_loop(2, 4, sample, 0)

    attn = attn_s[...].reshape(H, 8, 256)
    grad_attn = ga_s[...].reshape(H, 8, 256)
    inner = jnp.sum(attn * grad_attn, axis=1, keepdims=True)
    grad_logits = (attn * (grad_attn - inner)).reshape(64, 256)
    part_attn = dot(grad_logits.astype(BF16), column_feats[0])
    part_out = dot(mixed_s[...], grad_out[0])

    for q in range(NP):
        lanes = slice((q // 4) * 128, (q // 4 + 1) * 128)
        k = q % 4
        other_plane[q, 0:64] = part_out[k * 64:(k + 1) * 64, lanes].astype(BF16)
        other_plane[q, 64:80] = part_attn[k * 16:(k + 1) * 16, lanes].astype(BF16)
    share_out(1)
    along_z(0)
    grad_query = dot(grad_logits.T.astype(BF16), w_attn_t[...])
    along_x(1)
    chain_step(2)
    along_z(1)
    share_back(0)
    chain_step(3)
    share_back(1)
    own = acc[0]
    for side in range(2):
        for half in range(2):
            arrive(("chain", side, 3, half))
        own = own + rs_recv[side, 3].astype(F32)
    lay_rows(own)
    grad_values = jnp.concatenate([gv_rows[0:256].T, gv_rows[256:512].T], axis=0).astype(BF16)
    grad_feats[0] = (grad_query + dot(grad_values, w_value_t[...])).astype(BF16)
    arrive(3)
    value_sums[...] = value_all[...]
    arrive(7)
    other_sums[...] = other_all[...]

    settle()


def finish(grad_in, value_sums, other_sums, grad_feats, grad_w_value, grad_w_attn_t, grad_w_out):
    factor = 1.0 / math.sqrt(NX * NZ * NP * 256)
    grad_feats[...] = grad_in[...]
    for q in range(NP):
        lanes = slice((q // 4) * 128, (q // 4 + 1) * 128)
        k = q % 4
        grad_w_value[k * 64:(k + 1) * 64, lanes] = value_sums[q].astype(F32) * factor
        grad_w_out[k * 64:(k + 1) * 64, lanes] = other_sums[q, 0:64].astype(F32) * factor
        grad_w_attn_t[k * 16:(k + 1) * 16, lanes] = other_sums[q, 64:80].astype(F32) * factor


def per_device(feats, routes, interp, w_value, w_attn, w_out, grad_out):
    vmem = pl.BlockSpec(memory_space=pltpu.VMEM)
    dma = pltpu.SemaphoreType.DMA
    moved, value_sums, other_sums = pl.pallas_call(
        kernel,
        out_shape=(
            jax.ShapeDtypeStruct((1, 256, 256), BF16),
            jax.ShapeDtypeStruct((NP, SHARES[0], 128), BF16),
            jax.ShapeDtypeStruct((NP, SHARES[1], 128), BF16),
        ),
        in_specs=[pl.BlockSpec(memory_space=pltpu.HBM)] * 7,
        out_specs=(vmem,) * 3,
        scratch_shapes=[
            pltpu.VMEM((8, 256, 256), BF16),
            pltpu.VMEM((1, 64, 64), jnp.int32),
            pltpu.VMEM((256, 256), BF16),
            pltpu.VMEM((64, 256), BF16),
            pltpu.VMEM((256, 256), BF16),
            pltpu.VMEM((1, 256, 256), BF16),
            pltpu.VMEM((64, 256, 128), BF16),
            pltpu.VMEM((2, 256, 128), F32),
            pltpu.VMEM((8, 128, 512), BF16),
            pltpu.VMEM((8, 128, 512), BF16),
            pltpu.VMEM((8, 128, 512), BF16),
            pltpu.VMEM((8, 128, 512), BF16),
            pltpu.VMEM((8, 128, 512), BF16),
            pltpu.VMEM((8, 128, 512), F32),
            pltpu.VMEM((2, 4, 128, 512), BF16),
            pltpu.VMEM((2, 4, 128, 512), BF16),
            pltpu.VMEM((256, 128), F32),
            pltpu.VMEM((512, 512), BF16),
            pltpu.VMEM((512, 128), F32),
            pltpu.VMEM((512, 512), F32),
            pltpu.VMEM((64, 256), F32),
            pltpu.VMEM((256, 256), F32),
            pltpu.VMEM((64, 256), F32),
            pltpu.VMEM((256, 256), BF16),
            pltpu.VMEM((256, 256), BF16),
            pltpu.VMEM((256, 256), F32),
            pltpu.VMEM((8, 128, 128), BF16),
            pltpu.VMEM((8, 128, 128), BF16),
            pltpu.VMEM((8, 128, 512), BF16),
            pltpu.VMEM((512, 1024), BF16),
            pltpu.VMEM((8, 128), jnp.int32),
            pltpu.VMEM((512, 128), F32),
            *[
                pltpu.VMEM((count, rows, 128), BF16)
                for rows in SHARES
                for count in (NP, NP, NX, NZ, NP)
            ],
            dma((6,)),
            dma((H,)),
            dma((2, 4, 2)),
            dma((2, 4, 2)),
            dma((5,)),
            dma((5,)),
            dma((5,)),
            dma((5,)),
            dma((2, 4, 2)),
            dma((2, 4, 2)),
            dma((8,)),
            dma((8,)),
        ],
        compiler_params=pltpu.CompilerParams(
            collective_id=0, has_side_effects=True, vmem_limit_bytes=63 * 1024 * 1024
        ),
    )(feats, routes, interp, w_value, w_attn.T, w_out, grad_out)
    grads = pl.pallas_call(
        finish,
        out_shape=(
            jax.ShapeDtypeStruct((1, 256, 256), BF16),
            jax.ShapeDtypeStruct((256, 256), F32),
            jax.ShapeDtypeStruct((64, 256), F32),
            jax.ShapeDtypeStruct((256, 256), F32),
        ),
        in_specs=[vmem] * 3,
        out_specs=(vmem,) * 4,
    )(moved, value_sums, other_sums)
    return grads[0], grads[1], grads[2].T, grads[3]


def solution(mesh):
    in_specs = (
        P("frame", "tile", None),
        P("frame", None, None),
        P("frame", None, "tile", None),
        P(),
        P(),
        P(),
        P("frame", "tile", None),
    )
    out_specs = (P("frame", "tile", None), P(), P(), P())
    return jax.shard_map(
        per_device, mesh=mesh, in_specs=in_specs, out_specs=out_specs, check_vma=False
    )
```

```python
import math

import jax
import jax.numpy as jnp
from jax import lax
from jax.experimental import pallas as pl
from jax.experimental.pallas import tpu as pltpu
from jax.sharding import PartitionSpec as P

MESH = pl.DeviceIdType.MESH
F32 = jnp.float32
BF16 = jnp.bfloat16
NZ = 8
NP = 8
NX = 4
H = 8
SHARES = (64, 80)
PLACE = {0: 0, 1: 1, 7: 2, 2: 3, 6: 4, 3: 5, 5: 6, 4: 7}
GROUPS = ((0, 1), (1, 2), (3, 2), (5, 2), (7, 1))
NN = (((1,), (0,)), ((), ()))
NT = (((1,), (1,)), ((), ()))


def dot(a, b, dims=NN):
    return lax.dot_general(a, b, dims, preferred_element_type=F32)


def block(index, size):
    return pl.ds(pl.multiple_of(index * size, size), size)


def one_hot(hit):
    return jnp.where(hit, 1.0, 0.0).astype(BF16)


def kernel(
    feats_hbm, routes_hbm, interp, w_value_hbm, w_attn_hbm, w_out_hbm, grad_out_hbm,
    grad_feats, value_sums, other_sums,
    column_feats, routes, w_value, w_attn_t, w_out, grad_out, itp, itp_t, v_rows,
    maps, send_f, recv_f, send_r, recv_r, acc, rs_send, rs_recv,
    con, con_rows, fet, fetched, attn_s, gm_s, ga_s, mixed_s, w_value_t, value_s,
    pick_f, pick_r, mine_t, mine, route_s, gv_rows,
    value_plane, value_in, value_x, value_z, value_all,
    other_plane, other_in, other_x, other_z, other_all,
    in_sem, itp_sem, ag_send_sem, ag_recv_sem, f_send_sem, f_recv_sem,
    r_send_sem, r_recv_sem, rs_send_sem, rs_recv_sem, sum_send_sem, sum_recv_sem,
):
    t = lax.axis_index("tile")
    f = lax.axis_index("frame")
    z = lax.div(t, NP)
    p = lax.rem(t, NP)

    def plane_tile(i):
        return z * NP + lax.rem(p + i, NP)

    def column_tile(i):
        return lax.rem(z + i, NZ) * NP + p

    right = column_tile(1)
    left = column_tile(NZ - 1)

    leaving, coming = [], {}

    def remote(src, dst, send_sem, recv_sem, tile, frame):
        return pltpu.make_async_remote_copy(
            src_ref=src, dst_ref=dst, send_sem=send_sem, recv_sem=recv_sem,
            device_id=(tile, frame), device_id_type=MESH,
        )

    def send(key, copy):
        copy.start()
        leaving.append(copy.wait_send)
        coming[key] = copy.wait_recv

    def send_many(key, copies, size, send_sem, recv_sem):
        for copy in copies:
            copy.start()
        leaving.append(pltpu.make_async_copy(size, size, send_sem).wait)
        coming[key] = pltpu.make_async_copy(size, size, recv_sem).wait

    def arrive(key):
        coming.pop(key)()

    def settle():
        for key in list(coming):
            arrive(key)
        for wait in leaving:
            wait()

    barrier = pltpu.get_barrier_semaphore()
    near = [(plane_tile(i), f) for i in range(1, NP)] + [(right, f), (left, f)]
    near += [(t, lax.rem(f + i, NX)) for i in range(1, NX)]
    for device in near:
        pl.semaphore_signal(barrier, inc=1, device_id=device, device_id_type=MESH)

    ins = [
        pltpu.make_async_copy(src, dst, in_sem.at[i])
        for i, (src, dst) in enumerate((
            (feats_hbm.at[0], column_feats.at[0]), (w_value_hbm, w_value), (routes_hbm, routes),
            (w_attn_hbm, w_attn_t), (w_out_hbm, w_out), (grad_out_hbm, grad_out),
        ))
    ]
    loads = [
        pltpu.make_async_copy(
            interp.at[0, pl.ds(h * 8, 8)], itp.at[pl.ds(h * 8, 8)], itp_sem.at[h]
        )
        for h in range(H)
    ]
    for load in ins + loads:
        load.start()

    def value_maps(q):
        for l in range(2):
            v_rows[l] = dot(w_value_t[...], column_feats[q, l * 128:(l + 1) * 128, :], NT)
            for h in range(0, 8, 2):
                for c in range(4):
                    tiles = [v_rows[l, pl.ds((h + m) * 32 + c, 8, stride=4), :] for m in range(2)]
                    rows = slice(l * 64 + h * 8, l * 64 + h * 8 + 16)
                    maps[q, rows, c * 128:(c + 1) * 128] = jnp.concatenate(tiles, axis=0).astype(BF16)

    for load in ins:
        load.wait()

    route_s[...] = jnp.full(route_s.shape, -1, jnp.int32)
    route_s[:, 0:64] = routes[0, block(z, NP), :]
    row = lax.broadcasted_iota(jnp.int32, (128, 128), 0)
    lane = lax.broadcasted_iota(jnp.int32, (128, 128), 1)
    place = lax.div(row, 16)
    distance = jnp.where(lax.rem(place, 2) == 1, lax.div(place + 1, 2), NZ - lax.div(place, 2))
    row_slot = lax.rem(row, 2)
    row_plane = lax.rem(lax.div(row, 2), NP)
    owner_z = lax.rem(z + distance, NZ) * NP

    def picks(named, owner):
        hit = named == owner
        first = jnp.min(jnp.where(hit, lane, 128), axis=1, keepdims=True)
        is_first = jnp.where(lane == first, 1, 0)
        return jnp.where(hit & (is_first == 1 - row_slot), 1.0, 0.0).astype(F32)

    def same_row(shape):
        return lax.rem(lax.broadcasted_iota(jnp.int32, shape, 0), 8) == lax.rem(
            lax.broadcasted_iota(jnp.int32, shape, 1), 8
        )

    def by_eight(x):
        return jnp.broadcast_to(x[:, None, :], (x.shape[0], 8, x.shape[1])).reshape(x.shape[0] * 8, x.shape[1])

    def eighth(shape):
        return one_hot(
            lax.div(lax.broadcasted_iota(jnp.int32, shape, 1), 8) == lax.broadcasted_iota(jnp.int32, shape, 0)
        )

    mine_now = picks(jnp.broadcast_to(route_s[pl.ds(p, 1), :], (128, 128)), owner_z + row_plane)
    mine_wide = dot(mine_now.astype(BF16), eighth((128, 512)))
    keep_wide = same_row((128, 512))
    for q in range(8):
        mine_t[q] = jnp.where(keep_wide, by_eight(mine_wide[q * 16:(q + 1) * 16]), 0.0).astype(BF16)

    logits = dot(w_attn_t[...], column_feats[0], NT).reshape(H, 8, 256)
    powers = jnp.exp(logits - jnp.max(logits, axis=1, keepdims=True))
    attn_s[...] = (powers / jnp.sum(powers, axis=1, keepdims=True)).reshape(64, 256)
    gm_s[...] = dot(w_out[...], grad_out[0], NT)

    for load in loads:
        load.wait()

    def contribute(h, _):
        grad_mixed = gm_s[block(h, 32), :]
        weights = attn_s[block(h, 8), :]
        for i in range(8):
            grad_sampled = (weights[i:i + 1] * grad_mixed).astype(BF16)
            con[i * 32:(i + 1) * 32, :] = dot(grad_sampled, itp[h * 8 + i])
        for i in range(0, 8, 2):
            for c in range(4):
                tiles = [con[pl.ds((i + m) * 32 + c, 8, stride=4), :] for m in range(2)]
                con_rows[block(h * 4 + i // 2, 16), c * 128:(c + 1) * 128] = jnp.concatenate(tiles, axis=0).astype(BF16)
        return 0
    lax.fori_loop(0, H, contribute, 0)

    def choose(q, _):
        send_r[q] = dot(mine_t[q], con_rows[...]).astype(BF16)
        return 0
    lax.fori_loop(0, 8, choose, 0)

    def answer(q):
        send_f[q] = dot(pick_f[q], maps[q]).astype(BF16)
    pl.semaphore_wait(barrier, len(near))

    def ring(side, s, half):
        if side == 0:
            src, dst, to = (NZ - s) % NZ, NZ - 1 - s, right
        else:
            src, dst, to = s, s + 1, left
        rows = pl.ds(half * 128, 128)
        return remote(
            column_feats.at[PLACE[src], rows], column_feats.at[PLACE[dst], rows],
            ag_send_sem.at[side, s, half], ag_recv_sem.at[side, s, half], to, f,
        )

    ring_steps = [
        [(side, s, half) for order in range(2) for side in range(2)
         for half in ((side + order) % 2,) if s < 3 or half == side]
        for s in range(4)
    ]
    for step in ring_steps[0]:
        send(("ring", *step), ring(*step))

    def plane_send(name, src, dst, send_sem, recv_sem, g):
        first, count = GROUPS[g]
        blocks = pl.ds(first, count)
        copies = [
            remote(
                src.at[blocks, block(lax.rem(p + i, NP), 16)], dst.at[blocks, block(p, 16)],
                send_sem.at[g], recv_sem.at[g], plane_tile(i), f,
            )
            for i in range(1, NP)
        ]
        send_many((name, g), copies, dst.at[blocks, pl.ds(0, 16 * (NP - 1))], send_sem.at[g], recv_sem.at[g])
        for q in range(first, first + count):
            dst[q, block(p, 16), :] = src[q, block(p, 16), :]

    for g in range(5):
        plane_send("r", send_r, recv_r, r_send_sem, r_recv_sem, g)

    w_value_t[...] = w_value[...].astype(F32).T.astype(BF16)
    value_maps(0)
    mine_wide_t = dot(mine_now.T[0:64].astype(BF16), eighth((128, 1024)))
    readers = jnp.broadcast_to(
        jnp.broadcast_to(route_s[...][:, None, :], (8, 2, 128)).reshape(16, 128)[None], (8, 16, 128)
    ).reshape(128, 128)
    asked = picks(readers, owner_z + p)
    piece_of = lax.rem(lax.div(row, 4), 2) * 8 + lax.div(row, 8)
    to_piece = dot(asked.astype(BF16), one_hot(piece_of == lax.div(lane, 8)))
    keep = same_row((128, 128))
    keep_long = same_row((512, 128))
    for q in range(8):
        mine[:, q * 128:(q + 1) * 128] = jnp.where(
            keep_long, by_eight(mine_wide_t[:, q * 128:(q + 1) * 128]), 0.0
        ).astype(BF16)
        piece = jnp.where(keep, by_eight(to_piece[q * 16:(q + 1) * 16]), 0.0)
        pick_f[q] = piece.astype(BF16)
        pick_r[q] = piece.T.astype(BF16)
    answer(0)
    plane_send("f", send_f, recv_f, f_send_sem, f_recv_sem, 0)

    def chain(side, s, half):
        rows = pl.ds(half * 64, 64)
        return remote(
            rs_send.at[side, s, rows], rs_recv.at[side, s, rows],
            rs_send_sem.at[side, s, half], rs_recv_sem.at[side, s, half],
            right if side == 0 else left, f,
        )

    def lay_rows(total):
        for k in range(16):
            for c in range(4):
                gv_rows[pl.ds(k * 32 + c, 8, stride=4), :] = total[k * 8:(k + 1) * 8, c * 128:(c + 1) * 128]

    def add_up(g):
        arrive(("r", g))
        for q in range(GROUPS[g][0], GROUPS[g][0] + GROUPS[g][1]):
            total = dot(pick_r[q], recv_r[q])
            acc[q] = total
            lay_rows(total)
            part = dot(gv_rows[0:256].astype(BF16), column_feats[q, 0:128, :])
            part = part + dot(gv_rows[256:512].astype(BF16), column_feats[q, 128:256, :])
            value_s[...] = part if q == 0 else value_s[...] + part

    def chain_send(side, s, half):
        rows = slice(half * 64, half * 64 + 64)
        total = acc[PLACE[4 - s if side == 0 else 4 + s], rows]
        if s > 1 or (s == 1 and half == side):
            arrive(("chain", side, s - 1, half))
            total = total + rs_recv[side, s - 1, rows].astype(F32)
        rs_send[side, s, rows] = total.astype(BF16)
        send(("chain", side, s, half), chain(side, s, half))

    def chain_step(s):
        for order in range(2):
            for side in range(2):
                half = (1 - side + order) % 2
                if s > 0 or half == side:
                    chain_send(side, s, half)

    def turn(j, _):
        itp_t[j] = itp[j].T
        return 0

    for s in range(1, 4):
        for side, _, half in ring_steps[s - 1]:
            arrive(("ring", side, s - 1, half))
            if (side, s, half) in ring_steps[s]:
                send(("ring", side, s, half), ring(side, s, half))
        for q in range(GROUPS[s][0], GROUPS[s][0] + 2):
            value_maps(q)
            answer(q)
        plane_send("f", send_f, recv_f, f_send_sem, f_recv_sem, s)
        add_up(s - 1)
        lax.fori_loop((s - 1) * 22, min(s * 22, 64), turn, 0)
    for step in ring_steps[3]:
        arrive(("ring", *step))
    value_maps(7)
    answer(7)
    plane_send("f", send_f, recv_f, f_send_sem, f_recv_sem, 4)
    add_up(4)
    chain_step(0)
    add_up(3)
    part_value = value_s[...].T

    def exchange(key, count, src, dst, here, device):
        send_sem, recv_sem = sum_send_sem.at[key], sum_recv_sem.at[key]
        copies = [remote(src(i), dst.at[here], send_sem, recv_sem, *device(i)) for i in range(1, count)]
        send_many(key, copies, dst.at[pl.ds(0, count - 1)], send_sem, recv_sem)

    def added(ref, count):
        total = ref[0].astype(F32)
        for q in range(1, count):
            total = total + ref[q].astype(F32)
        return total.astype(BF16)

    stages = (
        (value_plane, value_in, value_x, value_z, value_all),
        (other_plane, other_in, other_x, other_z, other_all),
    )

    def share_out(n):
        plane, inward = stages[n][0:2]
        exchange(
            n * 4, NP, lambda i: plane.at[lax.rem(p + i, NP)], inward, p, lambda i: (plane_tile(i), f)
        )
        inward[p] = plane[p]

    def along_x(n):
        arrive(n * 4)
        across = stages[n][2]
        across[f] = added(stages[n][1], NP)
        exchange(n * 4 + 1, NX, lambda i: across.at[f], across, f, lambda i: (t, lax.rem(f + i, NX)))

    def along_z(n):
        arrive(n * 4 + 1)
        up = stages[n][3]
        up[z] = added(stages[n][2], NX)
        exchange(n * 4 + 2, NZ, lambda i: up.at[z], up, z, lambda i: (column_tile(i), f))

    def share_back(n):
        arrive(n * 4 + 2)
        back = stages[n][4]
        back[p] = added(stages[n][3], NZ)
        exchange(n * 4 + 3, NP, lambda i: back.at[p], back, p, lambda i: (plane_tile(i), f))

    for q in range(NP):
        lanes = slice((q // 4) * 128, (q // 4 + 1) * 128)
        k = q % 4
        value_plane[q] = part_value[k * 64:(k + 1) * 64, lanes].astype(BF16)
    share_out(0)

    for g in range(4):
        arrive(("f", g))
    near_rows = recv_f[0:7].reshape(7 * 128, 512)

    def fetch(e, _):
        fetched[block(e, 128), :] = dot(mine[block(e, 128), 0:896], near_rows)
        return 0
    lax.fori_loop(0, 4, fetch, 0)
    arrive(("f", 4))

    def sample(e, _):
        rows = fetched[block(e, 128), :] + dot(mine[block(e, 128), 896:1024], recv_f[7])
        for i in range(16):
            for c in range(4):
                fet[pl.ds(i * 32 + c, 8, stride=4), :] = rows[i * 8:(i + 1) * 8, c * 128:(c + 1) * 128]
        for m in range(2):
            h = e * 2 + m
            grad_mixed = gm_s[block(h, 32), :]
            weights = attn_s[block(h, 8), :]
            mixed = jnp.zeros((32, 256), F32)
            grads = []
            for i in range(8):
                k = m * 8 + i
                sampled = dot(fet[k * 32:(k + 1) * 32, :].astype(BF16), itp_t[h * 8 + i])
                mixed = mixed + weights[i:i + 1] * sampled
                grads.append(jnp.sum(grad_mixed * sampled, axis=0, keepdims=True))
            mixed_s[block(h, 32), :] = mixed.astype(BF16)
            ga_s[block(h, 8), :] = jnp.concatenate(grads, axis=0)
        return 0
    lax.fori_loop(0, 2, sample, 0)
    along_x(0)
    chain_step(1)
    lax.fori_loop(2, 4, sample, 0)

    attn = attn_s[...].reshape(H, 8, 256)
    grad_attn = ga_s[...].reshape(H, 8, 256)
    inner = jnp.sum(attn * grad_attn, axis=1, keepdims=True)
    grad_logits = (attn * (grad_attn - inner)).reshape(64, 256)
    part_attn = dot(grad_logits.astype(BF16), column_feats[0])
    part_out = dot(mixed_s[...], grad_out[0])

    for q in range(NP):
        lanes = slice((q // 4) * 128, (q // 4 + 1) * 128)
        k = q % 4
        other_plane[q, 0:64] = part_out[k * 64:(k + 1) * 64, lanes].astype(BF16)
        other_plane[q, 64:80] = part_attn[k * 16:(k + 1) * 16, lanes].astype(BF16)
    share_out(1)
    along_z(0)
    grad_query = dot(grad_logits.T.astype(BF16), w_attn_t[...])
    along_x(1)
    chain_step(2)
    along_z(1)
    share_back(0)
    chain_step(3)
    share_back(1)
    own = acc[0]
    for side in range(2):
        for half in range(2):
            arrive(("chain", side, 3, half))
        own = own + rs_recv[side, 3].astype(F32)
    lay_rows(own)
    grad_values = jnp.concatenate([gv_rows[0:256].T, gv_rows[256:512].T], axis=0).astype(BF16)
    grad_feats[0] = (grad_query + dot(grad_values, w_value_t[...])).astype(BF16)
    arrive(3)
    value_sums[...] = value_all[...]
    arrive(7)
    other_sums[...] = other_all[...]

    settle()


def finish(grad_in, value_sums, other_sums, grad_feats, grad_w_value, grad_w_attn_t, grad_w_out):
    factor = 1.0 / math.sqrt(NX * NZ * NP * 256)
    grad_feats[...] = grad_in[...]
    for q in range(NP):
        lanes = slice((q // 4) * 128, (q // 4 + 1) * 128)
        k = q % 4
        grad_w_value[k * 64:(k + 1) * 64, lanes] = value_sums[q].astype(F32) * factor
        grad_w_out[k * 64:(k + 1) * 64, lanes] = other_sums[q, 0:64].astype(F32) * factor
        grad_w_attn_t[k * 16:(k + 1) * 16, lanes] = other_sums[q, 64:80].astype(F32) * factor


def per_device(feats, routes, interp, w_value, w_attn, w_out, grad_out):
    vmem = pl.BlockSpec(memory_space=pltpu.VMEM)
    dma = pltpu.SemaphoreType.DMA
    moved, value_sums, other_sums = pl.pallas_call(
        kernel,
        out_shape=(
            jax.ShapeDtypeStruct((1, 256, 256), BF16),
            jax.ShapeDtypeStruct((NP, SHARES[0], 128), BF16),
            jax.ShapeDtypeStruct((NP, SHARES[1], 128), BF16),
        ),
        in_specs=[pl.BlockSpec(memory_space=pltpu.HBM)] * 7,
        out_specs=(vmem,) * 3,
        scratch_shapes=[
            pltpu.VMEM((8, 256, 256), BF16),
            pltpu.VMEM((1, 64, 64), jnp.int32),
            pltpu.VMEM((256, 256), BF16),
            pltpu.VMEM((64, 256), BF16),
            pltpu.VMEM((256, 256), BF16),
            pltpu.VMEM((1, 256, 256), BF16),
            pltpu.VMEM((64, 256, 128), BF16),
            pltpu.VMEM((64, 128, 256), BF16),
            pltpu.VMEM((2, 256, 128), F32),
            pltpu.VMEM((8, 128, 512), BF16),
            pltpu.VMEM((8, 128, 512), BF16),
            pltpu.VMEM((8, 128, 512), BF16),
            pltpu.VMEM((8, 128, 512), BF16),
            pltpu.VMEM((8, 128, 512), BF16),
            pltpu.VMEM((8, 128, 512), F32),
            pltpu.VMEM((2, 4, 128, 512), BF16),
            pltpu.VMEM((2, 4, 128, 512), BF16),
            pltpu.VMEM((256, 128), F32),
            pltpu.VMEM((512, 512), BF16),
            pltpu.VMEM((512, 128), F32),
            pltpu.VMEM((512, 512), F32),
            pltpu.VMEM((64, 256), F32),
            pltpu.VMEM((256, 256), F32),
            pltpu.VMEM((64, 256), F32),
            pltpu.VMEM((256, 256), BF16),
            pltpu.VMEM((256, 256), BF16),
            pltpu.VMEM((256, 256), F32),
            pltpu.VMEM((8, 128, 128), BF16),
            pltpu.VMEM((8, 128, 128), BF16),
            pltpu.VMEM((8, 128, 512), BF16),
            pltpu.VMEM((512, 1024), BF16),
            pltpu.VMEM((8, 128), jnp.int32),
            pltpu.VMEM((512, 128), F32),
            *[
                pltpu.VMEM((count, rows, 128), BF16)
                for rows in SHARES
                for count in (NP, NP, NX, NZ, NP)
            ],
            dma((6,)),
            dma((H,)),
            dma((2, 4, 2)),
            dma((2, 4, 2)),
            dma((5,)),
            dma((5,)),
            dma((5,)),
            dma((5,)),
            dma((2, 4, 2)),
            dma((2, 4, 2)),
            dma((8,)),
            dma((8,)),
        ],
        compiler_params=pltpu.CompilerParams(
            collective_id=0, has_side_effects=True, vmem_limit_bytes=63 * 1024 * 1024
        ),
    )(feats, routes, interp, w_value, w_attn.T, w_out, grad_out)
    grads = pl.pallas_call(
        finish,
        out_shape=(
            jax.ShapeDtypeStruct((1, 256, 256), BF16),
            jax.ShapeDtypeStruct((256, 256), F32),
            jax.ShapeDtypeStruct((64, 256), F32),
            jax.ShapeDtypeStruct((256, 256), F32),
        ),
        in_specs=[vmem] * 3,
        out_specs=(vmem,) * 4,
    )(moved, value_sums, other_sums)
    return grads[0], grads[1], grads[2].T, grads[3]


def solution(mesh):
    in_specs = (
        P("frame", "tile", None),
        P("frame", None, None),
        P("frame", None, "tile", None),
        P(),
        P(),
        P(),
        P("frame", "tile", None),
    )
    out_specs = (P("frame", "tile", None), P(), P(), P())
    return jax.shard_map(
        per_device, mesh=mesh, in_specs=in_specs, out_specs=out_specs, check_vma=False
    )
```

```python
import math

import jax
import jax.numpy as jnp
from jax import lax
from jax.experimental import pallas as pl
from jax.experimental.pallas import tpu as pltpu
from jax.sharding import PartitionSpec as P

MESH = pl.DeviceIdType.MESH
F32 = jnp.float32
BF16 = jnp.bfloat16
NZ = 8
NP = 8
NX = 4
H = 8
SHARES = (64, 80)
PLACE = {0: 0, 1: 1, 7: 2, 2: 3, 6: 4, 3: 5, 5: 6, 4: 7}
GROUPS = ((0, 1), (1, 2), (3, 2), (5, 2), (7, 1))
NN = (((1,), (0,)), ((), ()))
NT = (((1,), (1,)), ((), ()))


def dot(a, b, dims=NN):
    return lax.dot_general(a, b, dims, preferred_element_type=F32)


def block(index, size):
    return pl.ds(pl.multiple_of(index * size, size), size)


def one_hot(hit):
    return jnp.where(hit, 1.0, 0.0).astype(BF16)


def kernel(
    feats_hbm, routes_hbm, interp, w_value_hbm, w_attn_hbm, w_out_hbm, grad_out_hbm,
    grad_feats, value_sums, other_sums,
    column_feats, routes, w_value, w_attn_t, w_out, grad_out, itp, itp_t, v_rows,
    maps, send_f, recv_f, send_r, recv_r, acc, rs_send, rs_recv,
    con, con_rows, fet, fetched, attn_s, gm_s, ga_s, mixed_s, w_value_t, value_s,
    pick_f, pick_r, mine_t, mine, route_s, gv_rows,
    value_plane, value_in, value_x, value_z, value_all,
    other_plane, other_in, other_x, other_z, other_all,
    moved, in_sem, out_sem, itp_sem, ag_send_sem, ag_recv_sem, f_send_sem, f_recv_sem,
    r_send_sem, r_recv_sem, rs_send_sem, rs_recv_sem, sum_send_sem, sum_recv_sem,
):
    t = lax.axis_index("tile")
    f = lax.axis_index("frame")
    z = lax.div(t, NP)
    p = lax.rem(t, NP)

    def plane_tile(i):
        return z * NP + lax.rem(p + i, NP)

    def column_tile(i):
        return lax.rem(z + i, NZ) * NP + p

    right = column_tile(1)
    left = column_tile(NZ - 1)

    leaving, coming = [], {}

    def remote(src, dst, send_sem, recv_sem, tile, frame):
        return pltpu.make_async_remote_copy(
            src_ref=src, dst_ref=dst, send_sem=send_sem, recv_sem=recv_sem,
            device_id=(tile, frame), device_id_type=MESH,
        )

    def send(key, copy):
        copy.start()
        leaving.append(copy.wait_send)
        coming[key] = copy.wait_recv

    def send_many(key, copies, size, send_sem, recv_sem):
        for copy in copies:
            copy.start()
        leaving.append(pltpu.make_async_copy(size, size, send_sem).wait)
        coming[key] = pltpu.make_async_copy(size, size, recv_sem).wait

    def arrive(key):
        coming.pop(key)()

    def settle():
        for key in list(coming):
            arrive(key)
        for wait in leaving:
            wait()

    barrier = pltpu.get_barrier_semaphore()
    near = [(plane_tile(i), f) for i in range(1, NP)] + [(right, f), (left, f)]
    near += [(t, lax.rem(f + i, NX)) for i in range(1, NX)]
    for device in near:
        pl.semaphore_signal(barrier, inc=1, device_id=device, device_id_type=MESH)

    ins = [
        pltpu.make_async_copy(src, dst, in_sem.at[i])
        for i, (src, dst) in enumerate((
            (feats_hbm.at[0], column_feats.at[0]), (w_value_hbm, w_value), (routes_hbm, routes),
            (w_attn_hbm, w_attn_t), (w_out_hbm, w_out), (grad_out_hbm, grad_out),
        ))
    ]
    loads = [
        pltpu.make_async_copy(
            interp.at[0, pl.ds(h * 8, 8)], itp.at[pl.ds(h * 8, 8)], itp_sem.at[h]
        )
        for h in range(H)
    ]
    for load in ins + loads:
        load.start()

    def value_maps(q):
        for l in range(2):
            v_rows[l] = dot(w_value_t[...], column_feats[q, l * 128:(l + 1) * 128, :], NT)
            for h in range(0, 8, 2):
                for c in range(4):
                    tiles = [v_rows[l, pl.ds((h + m) * 32 + c, 8, stride=4), :] for m in range(2)]
                    rows = slice(l * 64 + h * 8, l * 64 + h * 8 + 16)
                    maps[q, rows, c * 128:(c + 1) * 128] = jnp.concatenate(tiles, axis=0).astype(BF16)

    for load in ins:
        load.wait()

    route_s[...] = jnp.full(route_s.shape, -1, jnp.int32)
    route_s[:, 0:64] = routes[0, block(z, NP), :]
    row = lax.broadcasted_iota(jnp.int32, (128, 128), 0)
    lane = lax.broadcasted_iota(jnp.int32, (128, 128), 1)
    place = lax.div(row, 16)
    distance = jnp.where(lax.rem(place, 2) == 1, lax.div(place + 1, 2), NZ - lax.div(place, 2))
    row_slot = lax.rem(row, 2)
    row_plane = lax.rem(lax.div(row, 2), NP)
    owner_z = lax.rem(z + distance, NZ) * NP

    def picks(named, owner):
        hit = named == owner
        first = jnp.min(jnp.where(hit, lane, 128), axis=1, keepdims=True)
        is_first = jnp.where(lane == first, 1, 0)
        return jnp.where(hit & (is_first == 1 - row_slot), 1.0, 0.0).astype(F32)

    def same_row(shape):
        return lax.rem(lax.broadcasted_iota(jnp.int32, shape, 0), 8) == lax.rem(
            lax.broadcasted_iota(jnp.int32, shape, 1), 8
        )

    def by_eight(x):
        return jnp.broadcast_to(x[:, None, :], (x.shape[0], 8, x.shape[1])).reshape(x.shape[0] * 8, x.shape[1])

    def eighth(shape):
        return one_hot(
            lax.div(lax.broadcasted_iota(jnp.int32, shape, 1), 8) == lax.broadcasted_iota(jnp.int32, shape, 0)
        )

    mine_now = picks(jnp.broadcast_to(route_s[pl.ds(p, 1), :], (128, 128)), owner_z + row_plane)
    mine_wide = dot(mine_now.astype(BF16), eighth((128, 512)))
    keep_wide = same_row((128, 512))
    for q in range(8):
        mine_t[q] = jnp.where(keep_wide, by_eight(mine_wide[q * 16:(q + 1) * 16]), 0.0).astype(BF16)

    logits = dot(w_attn_t[...], column_feats[0], NT).reshape(H, 8, 256)
    powers = jnp.exp(logits - jnp.max(logits, axis=1, keepdims=True))
    attn_s[...] = (powers / jnp.sum(powers, axis=1, keepdims=True)).reshape(64, 256)
    gm_s[...] = dot(w_out[...], grad_out[0], NT)

    for load in loads:
        load.wait()

    def contribute(h, _):
        grad_mixed = gm_s[block(h, 32), :]
        weights = attn_s[block(h, 8), :]
        for i in range(8):
            grad_sampled = (weights[i:i + 1] * grad_mixed).astype(BF16)
            con[i * 32:(i + 1) * 32, :] = dot(grad_sampled, itp[h * 8 + i])
        for i in range(0, 8, 2):
            for c in range(4):
                tiles = [con[pl.ds((i + m) * 32 + c, 8, stride=4), :] for m in range(2)]
                con_rows[block(h * 4 + i // 2, 16), c * 128:(c + 1) * 128] = jnp.concatenate(tiles, axis=0).astype(BF16)
        return 0
    lax.fori_loop(0, H, contribute, 0)

    def choose(q, _):
        send_r[q] = dot(mine_t[q], con_rows[...]).astype(BF16)
        return 0
    lax.fori_loop(0, 8, choose, 0)

    def answer(q):
        send_f[q] = dot(pick_f[q], maps[q]).astype(BF16)
    pl.semaphore_wait(barrier, len(near))

    def ring(side, s, half):
        if side == 0:
            src, dst, to = (NZ - s) % NZ, NZ - 1 - s, right
        else:
            src, dst, to = s, s + 1, left
        rows = pl.ds(half * 128, 128)
        return remote(
            column_feats.at[PLACE[src], rows], column_feats.at[PLACE[dst], rows],
            ag_send_sem.at[side, s, half], ag_recv_sem.at[side, s, half], to, f,
        )

    ring_steps = [
        [(side, s, half) for order in range(2) for side in range(2)
         for half in ((side + order) % 2,) if s < 3 or half == side]
        for s in range(4)
    ]
    for step in ring_steps[0]:
        send(("ring", *step), ring(*step))

    def plane_send(name, src, dst, send_sem, recv_sem, g):
        first, count = GROUPS[g]
        blocks = pl.ds(first, count)
        copies = [
            remote(
                src.at[blocks, block(lax.rem(p + i, NP), 16)], dst.at[blocks, block(p, 16)],
                send_sem.at[g], recv_sem.at[g], plane_tile(i), f,
            )
            for i in range(1, NP)
        ]
        send_many((name, g), copies, dst.at[blocks, pl.ds(0, 16 * (NP - 1))], send_sem.at[g], recv_sem.at[g])
        for q in range(first, first + count):
            dst[q, block(p, 16), :] = src[q, block(p, 16), :]

    for g in range(5):
        plane_send("r", send_r, recv_r, r_send_sem, r_recv_sem, g)

    w_value_t[...] = w_value[...].astype(F32).T.astype(BF16)
    value_maps(0)
    mine_wide_t = dot(mine_now.T[0:64].astype(BF16), eighth((128, 1024)))
    readers = jnp.broadcast_to(
        jnp.broadcast_to(route_s[...][:, None, :], (8, 2, 128)).reshape(16, 128)[None], (8, 16, 128)
    ).reshape(128, 128)
    asked = picks(readers, owner_z + p)
    piece_of = lax.rem(lax.div(row, 4), 2) * 8 + lax.div(row, 8)
    to_piece = dot(asked.astype(BF16), one_hot(piece_of == lax.div(lane, 8)))
    keep = same_row((128, 128))
    keep_long = same_row((512, 128))
    for q in range(8):
        mine[:, q * 128:(q + 1) * 128] = jnp.where(
            keep_long, by_eight(mine_wide_t[:, q * 128:(q + 1) * 128]), 0.0
        ).astype(BF16)
        piece = jnp.where(keep, by_eight(to_piece[q * 16:(q + 1) * 16]), 0.0)
        pick_f[q] = piece.astype(BF16)
        pick_r[q] = piece.T.astype(BF16)
    answer(0)
    plane_send("f", send_f, recv_f, f_send_sem, f_recv_sem, 0)

    def chain(side, s, half):
        rows = pl.ds(half * 64, 64)
        return remote(
            rs_send.at[side, s, rows], rs_recv.at[side, s, rows],
            rs_send_sem.at[side, s, half], rs_recv_sem.at[side, s, half],
            right if side == 0 else left, f,
        )

    def lay_rows(total):
        for k in range(16):
            for c in range(4):
                gv_rows[pl.ds(k * 32 + c, 8, stride=4), :] = total[k * 8:(k + 1) * 8, c * 128:(c + 1) * 128]

    def add_up(g):
        arrive(("r", g))
        for q in range(GROUPS[g][0], GROUPS[g][0] + GROUPS[g][1]):
            total = dot(pick_r[q], recv_r[q])
            acc[q] = total
            lay_rows(total)
            part = dot(gv_rows[0:256].astype(BF16), column_feats[q, 0:128, :])
            part = part + dot(gv_rows[256:512].astype(BF16), column_feats[q, 128:256, :])
            value_s[...] = part if q == 0 else value_s[...] + part

    def chain_send(side, s, half):
        rows = slice(half * 64, half * 64 + 64)
        total = acc[PLACE[4 - s if side == 0 else 4 + s], rows]
        if s > 1 or (s == 1 and half == side):
            arrive(("chain", side, s - 1, half))
            total = total + rs_recv[side, s - 1, rows].astype(F32)
        rs_send[side, s, rows] = total.astype(BF16)
        send(("chain", side, s, half), chain(side, s, half))

    def chain_step(s):
        for order in range(2):
            for side in range(2):
                half = (1 - side + order) % 2
                if s > 0 or half == side:
                    chain_send(side, s, half)

    def turn(j, _):
        itp_t[j] = itp[j].T
        return 0

    for s in range(1, 4):
        for side, _, half in ring_steps[s - 1]:
            arrive(("ring", side, s - 1, half))
            if (side, s, half) in ring_steps[s]:
                send(("ring", side, s, half), ring(side, s, half))
        for q in range(GROUPS[s][0], GROUPS[s][0] + 2):
            value_maps(q)
            answer(q)
        plane_send("f", send_f, recv_f, f_send_sem, f_recv_sem, s)
        add_up(s - 1)
        lax.fori_loop((s - 1) * 22, min(s * 22, 64), turn, 0)
    for step in ring_steps[3]:
        arrive(("ring", *step))
    value_maps(7)
    answer(7)
    plane_send("f", send_f, recv_f, f_send_sem, f_recv_sem, 4)
    add_up(4)
    chain_step(0)
    add_up(3)
    part_value = value_s[...].T

    def exchange(key, count, src, dst, here, device):
        send_sem, recv_sem = sum_send_sem.at[key], sum_recv_sem.at[key]
        copies = [remote(src(i), dst.at[here], send_sem, recv_sem, *device(i)) for i in range(1, count)]
        send_many(key, copies, dst.at[pl.ds(0, count - 1)], send_sem, recv_sem)

    def added(ref, count):
        total = ref[0].astype(F32)
        for q in range(1, count):
            total = total + ref[q].astype(F32)
        return total.astype(BF16)

    stages = (
        (value_plane, value_in, value_x, value_z, value_all),
        (other_plane, other_in, other_x, other_z, other_all),
    )

    def share_out(n):
        plane, inward = stages[n][0:2]
        exchange(
            n * 4, NP, lambda i: plane.at[lax.rem(p + i, NP)], inward, p, lambda i: (plane_tile(i), f)
        )
        inward[p] = plane[p]

    def along_x(n):
        arrive(n * 4)
        across = stages[n][2]
        across[f] = added(stages[n][1], NP)
        exchange(n * 4 + 1, NX, lambda i: across.at[f], across, f, lambda i: (t, lax.rem(f + i, NX)))

    def along_z(n):
        arrive(n * 4 + 1)
        up = stages[n][3]
        up[z] = added(stages[n][2], NX)
        exchange(n * 4 + 2, NZ, lambda i: up.at[z], up, z, lambda i: (column_tile(i), f))

    def share_back(n):
        arrive(n * 4 + 2)
        back = stages[n][4]
        back[p] = added(stages[n][3], NZ)
        exchange(n * 4 + 3, NP, lambda i: back.at[p], back, p, lambda i: (plane_tile(i), f))

    for q in range(NP):
        lanes = slice((q // 4) * 128, (q // 4 + 1) * 128)
        k = q % 4
        value_plane[q] = part_value[k * 64:(k + 1) * 64, lanes].astype(BF16)
    share_out(0)

    for g in range(4):
        arrive(("f", g))
    near_rows = recv_f[0:7].reshape(7 * 128, 512)

    def fetch(e, _):
        fetched[block(e, 128), :] = dot(mine[block(e, 128), 0:896], near_rows)
        return 0
    lax.fori_loop(0, 4, fetch, 0)
    arrive(("f", 4))

    def sample(e, _):
        rows = fetched[block(e, 128), :] + dot(mine[block(e, 128), 896:1024], recv_f[7])
        for i in range(16):
            for c in range(4):
                fet[pl.ds(i * 32 + c, 8, stride=4), :] = rows[i * 8:(i + 1) * 8, c * 128:(c + 1) * 128]
        for m in range(2):
            h = e * 2 + m
            grad_mixed = gm_s[block(h, 32), :]
            weights = attn_s[block(h, 8), :]
            mixed = jnp.zeros((32, 256), F32)
            grads = []
            for i in range(8):
                k = m * 8 + i
                sampled = dot(fet[k * 32:(k + 1) * 32, :].astype(BF16), itp_t[h * 8 + i])
                mixed = mixed + weights[i:i + 1] * sampled
                grads.append(jnp.sum(grad_mixed * sampled, axis=0, keepdims=True))
            mixed_s[block(h, 32), :] = mixed.astype(BF16)
            ga_s[block(h, 8), :] = jnp.concatenate(grads, axis=0)
        return 0
    lax.fori_loop(0, 2, sample, 0)
    along_x(0)
    chain_step(1)
    lax.fori_loop(2, 4, sample, 0)

    attn = attn_s[...].reshape(H, 8, 256)
    grad_attn = ga_s[...].reshape(H, 8, 256)
    inner = jnp.sum(attn * grad_attn, axis=1, keepdims=True)
    grad_logits = (attn * (grad_attn - inner)).reshape(64, 256)
    part_attn = dot(grad_logits.astype(BF16), column_feats[0])
    part_out = dot(mixed_s[...], grad_out[0])

    for q in range(NP):
        lanes = slice((q // 4) * 128, (q // 4 + 1) * 128)
        k = q % 4
        other_plane[q, 0:64] = part_out[k * 64:(k + 1) * 64, lanes].astype(BF16)
        other_plane[q, 64:80] = part_attn[k * 16:(k + 1) * 16, lanes].astype(BF16)
    share_out(1)
    along_z(0)
    grad_query = dot(grad_logits.T.astype(BF16), w_attn_t[...])
    along_x(1)
    chain_step(2)
    along_z(1)
    share_back(0)
    chain_step(3)
    share_back(1)
    own = acc[0]
    for side in range(2):
        for half in range(2):
            arrive(("chain", side, 3, half))
        own = own + rs_recv[side, 3].astype(F32)
    lay_rows(own)
    grad_values = jnp.concatenate([gv_rows[0:256].T, gv_rows[256:512].T], axis=0).astype(BF16)
    moved[...] = (grad_query + dot(grad_values, w_value_t[...])).astype(BF16)
    outs = [
        pltpu.make_async_copy(src, dst, out_sem.at[i])
        for i, (src, dst) in enumerate((
            (moved, grad_feats.at[0]), (value_all, value_sums), (other_all, other_sums),
        ))
    ]
    outs[0].start()
    arrive(3)
    outs[1].start()
    arrive(7)
    outs[2].start()
    for out in outs:
        out.wait()

    settle()


def finish(grad_in, value_sums, other_sums, grad_feats, grad_w_value, grad_w_attn_t, grad_w_out):
    factor = 1.0 / math.sqrt(NX * NZ * NP * 256)
    grad_feats[...] = grad_in[...]
    for q in range(NP):
        lanes = slice((q // 4) * 128, (q // 4 + 1) * 128)
        k = q % 4
        grad_w_value[k * 64:(k + 1) * 64, lanes] = value_sums[q].astype(F32) * factor
        grad_w_out[k * 64:(k + 1) * 64, lanes] = other_sums[q, 0:64].astype(F32) * factor
        grad_w_attn_t[k * 16:(k + 1) * 16, lanes] = other_sums[q, 64:80].astype(F32) * factor


def per_device(feats, routes, interp, w_value, w_attn, w_out, grad_out):
    vmem = pl.BlockSpec(memory_space=pltpu.VMEM)
    dma = pltpu.SemaphoreType.DMA
    moved, value_sums, other_sums = pl.pallas_call(
        kernel,
        out_shape=(
            jax.ShapeDtypeStruct((1, 256, 256), BF16),
            jax.ShapeDtypeStruct((NP, SHARES[0], 128), BF16),
            jax.ShapeDtypeStruct((NP, SHARES[1], 128), BF16),
        ),
        in_specs=[pl.BlockSpec(memory_space=pltpu.HBM)] * 7,
        out_specs=(pl.BlockSpec(memory_space=pl.ANY),) * 3,
        scratch_shapes=[
            pltpu.VMEM((8, 256, 256), BF16),
            pltpu.VMEM((1, 64, 64), jnp.int32),
            pltpu.VMEM((256, 256), BF16),
            pltpu.VMEM((64, 256), BF16),
            pltpu.VMEM((256, 256), BF16),
            pltpu.VMEM((1, 256, 256), BF16),
            pltpu.VMEM((64, 256, 128), BF16),
            pltpu.VMEM((64, 128, 256), BF16),
            pltpu.VMEM((2, 256, 128), F32),
            pltpu.VMEM((8, 128, 512), BF16),
            pltpu.VMEM((8, 128, 512), BF16),
            pltpu.VMEM((8, 128, 512), BF16),
            pltpu.VMEM((8, 128, 512), BF16),
            pltpu.VMEM((8, 128, 512), BF16),
            pltpu.VMEM((8, 128, 512), F32),
            pltpu.VMEM((2, 4, 128, 512), BF16),
            pltpu.VMEM((2, 4, 128, 512), BF16),
            pltpu.VMEM((256, 128), F32),
            pltpu.VMEM((512, 512), BF16),
            pltpu.VMEM((512, 128), F32),
            pltpu.VMEM((512, 512), F32),
            pltpu.VMEM((64, 256), F32),
            pltpu.VMEM((256, 256), F32),
            pltpu.VMEM((64, 256), F32),
            pltpu.VMEM((256, 256), BF16),
            pltpu.VMEM((256, 256), BF16),
            pltpu.VMEM((256, 256), F32),
            pltpu.VMEM((8, 128, 128), BF16),
            pltpu.VMEM((8, 128, 128), BF16),
            pltpu.VMEM((8, 128, 512), BF16),
            pltpu.VMEM((512, 1024), BF16),
            pltpu.VMEM((8, 128), jnp.int32),
            pltpu.VMEM((512, 128), F32),
            *[
                pltpu.VMEM((count, rows, 128), BF16)
                for rows in SHARES
                for count in (NP, NP, NX, NZ, NP)
            ],
            pltpu.VMEM((256, 256), BF16),
            dma((6,)),
            dma((3,)),
            dma((H,)),
            dma((2, 4, 2)),
            dma((2, 4, 2)),
            dma((5,)),
            dma((5,)),
            dma((5,)),
            dma((5,)),
            dma((2, 4, 2)),
            dma((2, 4, 2)),
            dma((8,)),
            dma((8,)),
        ],
        compiler_params=pltpu.CompilerParams(
            collective_id=0, has_side_effects=True, vmem_limit_bytes=63 * 1024 * 1024
        ),
    )(feats, routes, interp, w_value, w_attn.T, w_out, grad_out)
    grads = pl.pallas_call(
        finish,
        out_shape=(
            jax.ShapeDtypeStruct((1, 256, 256), BF16),
            jax.ShapeDtypeStruct((256, 256), F32),
            jax.ShapeDtypeStruct((64, 256), F32),
            jax.ShapeDtypeStruct((256, 256), F32),
        ),
        in_specs=[vmem] * 3,
        out_specs=(vmem,) * 4,
    )(moved, value_sums, other_sums)
    return grads[0], grads[1], grads[2].T, grads[3]


def solution(mesh):
    in_specs = (
        P("frame", "tile", None),
        P("frame", None, None),
        P("frame", None, "tile", None),
        P(),
        P(),
        P(),
        P("frame", "tile", None),
    )
    out_specs = (P("frame", "tile", None), P(), P(), P())
    return jax.shard_map(
        per_device, mesh=mesh, in_specs=in_specs, out_specs=out_specs, check_vma=False
    )
```
